128 devices in a mesh: expert: 2 (over z_lo), rep: 4 (over y), seq: 16 (over z_hi, x, core).
Axes of the slice: x: 4, y: 4, z: 4 (z_hi: 2, z_lo: 2; z = z_hi * 2 + z_lo), core: 2. Of those that a mesh axis runs over, the one named last changes fastest.
Arguments:
- query_in: bfloat16 [2, 8, 2048, 4096], P('expert', 'rep', 'seq'), may hold values from -64 to 64
- key_in: bfloat16 [2, 8, 2048, 4096], P('expert', 'rep', 'seq'), may hold values from -64 to 64
- value_in: bfloat16 [2, 8, 2048, 4096], P('expert', 'rep', 'seq'), may hold values from -12 to 12
- sample_noise: bfloat16 [2, 8, 2048, 4096], P('expert', 'rep', 'seq'), may hold values from -12 to 12
- old_velocity: bfloat16 [2, 8, 2048, 4096], P('expert', 'rep', 'seq'), may hold values from -12 to 12
- gate_scale: bfloat16 [2, 8, 4096], P('expert', 'rep'), may hold values from 0.5 to 1.5
- rewards: float32 [2, 8], P(None, 'rep'), may hold values from -12 to 12
- group_ids: int32 [2, 8], P(None, 'rep'), may hold values from 0 to 3
- timesteps: int32 [2, 8], P(None, 'rep'), may hold values from 150 to 899, as said below
- counts: int32 [2, 4], P(None, 'rep'), may hold values from 0 to 2, as said below
Outputs:
- grad_query: bfloat16 [2, 8, 2048, 4096], P('expert', 'rep', 'seq')
- grad_key: bfloat16 [2, 8, 2048, 4096], P('expert', 'rep', 'seq')
- grad_value: bfloat16 [2, 8, 2048, 4096], P('expert', 'rep', 'seq')
- grad_gate: bfloat16 [2, 8, 4096], P('expert', 'rep')
- log_ratio: bfloat16 [2, 8], P('expert', 'rep')
The draws below stay inside these ranges and needn't reach their ends.
Inputs may be any that keep to these rules, and one draw needn't show every extreme that they name: Steps of expert set 0 have timesteps of 875 or more, steps of set 1 below 875. `counts`: every replica of one expert set, chosen from the seed, keeps all 2 slots; some replica of the other set keeps none.
All inputs are finite; a program needn't handle non-finite values.
Results may differ from the reference program's by a relative error of at most 0.012.
The reference program's roundings to bfloat16 on the way (of `probabilities`, `attended`, `grad_attended` and `grad_scores`) count: a program that leaves them out, or rounds other values in their place, can miss the bound.
Values may be sent and summed in bfloat16 or wider, within the bound.
No kernel may reach another device: no remote copies, remote signals or barrier semaphores. Data moves between devices by JAX's collectives and lax.ppermute only.
A program may use at most 256 MiB of HBM per device.

```python
import jax
import jax.numpy as jnp
from jax import lax

HEADS = 32
HD = 128
SLOTS = 2
GROUPS = 4
SETS = 2
REPLICAS = 4
STEPS = 8
LEN = 2048
WIDTH = 4096


def draw_query_in(key, part):
    own_key = jax.random.fold_in(key, 11)
    array_shape = (SETS, STEPS, LEN, WIDTH)
    values = jax.random.normal(own_key, array_shape, jnp.float32)
    return values.astype(jnp.bfloat16)


def draw_key_in(key, part):
    own_key = jax.random.fold_in(key, 12)
    array_shape = (SETS, STEPS, LEN, WIDTH)
    values = jax.random.normal(own_key, array_shape, jnp.float32)
    return values.astype(jnp.bfloat16)


def draw_value_in(key, part):
    own_key = jax.random.fold_in(key, 13)
    array_shape = (SETS, STEPS, LEN, WIDTH)
    values = jax.random.normal(own_key, array_shape, jnp.float32)
    return values.astype(jnp.bfloat16)


def rising_field(own_key):
    array_shape = (SETS, STEPS, LEN, WIDTH)
    rising = 0.5 + jnp.arange(LEN, dtype=jnp.float32) / LEN
    values = jax.random.normal(own_key, array_shape, jnp.float32) * rising[:, None]
    return values.astype(jnp.bfloat16)


def draw_sample_noise(key, part):
    own_key = jax.random.fold_in(key, 17)
    return rising_field(own_key)


def draw_old_velocity(key, part):
    own_key = jax.random.fold_in(key, 19)
    return rising_field(own_key)


def draw_rewards(key, part):
    own_key = jax.random.fold_in(key, 23)
    rising = 0.5 + jnp.arange(STEPS, dtype=jnp.float32) / STEPS
    values = jax.random.normal(own_key, (SETS, STEPS), jnp.float32) * rising[None, :]
    return values


def draw_timesteps(key, part):
    own_key = jax.random.fold_in(key, 29)
    first_key, second_key = jax.random.split(own_key)
    high_noise = jax.random.randint(first_key, (1, STEPS), 875, 900)
    low_noise = jax.random.randint(second_key, (1, STEPS), 150, 875)
    return jnp.concatenate([high_noise, low_noise], axis=0).astype(jnp.int32)


def draw_counts(key, part):
    own_key = jax.random.fold_in(key, 31)
    first_key, second_key, third_key = jax.random.split(own_key, 3)
    busy_set = jax.random.randint(first_key, (), 0, 2)
    partner_counts = jax.random.randint(second_key, (REPLICAS,), 0, SLOTS + 1)
    empty_replica = jax.random.randint(third_key, (), 0, REPLICAS)
    partner_counts = jnp.where(jnp.arange(REPLICAS) == empty_replica, 0, partner_counts)
    set_index = jnp.arange(2)[:, None]
    return jnp.where(set_index == busy_set, SLOTS, partner_counts[None, :]).astype(jnp.int32)


def place_ends(entries, key, smallest, top_value):
    longest = entries.shape.index(max(entries.shape))
    spots = []
    for shift in (0, 1):
        where = [jax.random.randint(jax.random.fold_in(key, axis), (), 0, length) for axis, length in enumerate(entries.shape)]
        where[longest] = (where[longest] + shift) % entries.shape[longest]
        spots.append(tuple(where))
    return entries.at[spots[0]].set(smallest).at[spots[1]].set(top_value)


def setup_inputs(seed: int = 0) -> dict:
    keys = jax.random.split(jax.random.key(seed), 11)
    query_in = draw_query_in(jax.random.fold_in(keys[10], 71), 0)
    key_in = draw_key_in(jax.random.fold_in(keys[10], 71), 0)
    value_in = draw_value_in(jax.random.fold_in(keys[10], 71), 0)
    sample_noise = draw_sample_noise(jax.random.fold_in(keys[10], 71), 0)
    old_velocity = draw_old_velocity(jax.random.fold_in(keys[10], 71), 0)
    gate_scale = jnp.clip(1.0 + 0.1 * jax.random.normal(keys[5], (SETS, STEPS, WIDTH), jnp.float32), 0.5, 1.5).astype(jnp.bfloat16)
    rewards = draw_rewards(jax.random.fold_in(keys[10], 71), 0)
    group_ids = place_ends(jax.random.randint(keys[7], (SETS, STEPS), 0, GROUPS), jax.random.fold_in(keys[7], 1), 0, GROUPS - 1).astype(jnp.int32)
    timesteps = draw_timesteps(jax.random.fold_in(keys[10], 71), 0)
    counts = draw_counts(jax.random.fold_in(keys[10], 71), 0)
    return {"query_in": query_in, "key_in": key_in, "value_in": value_in, "sample_noise": sample_noise, "old_velocity": old_velocity, "gate_scale": gate_scale, "rewards": rewards, "group_ids": group_ids, "timesteps": timesteps, "counts": counts}


def step_coef(timesteps):
    fraction = timesteps.astype(jnp.float32) / 1000.0
    sigma_level = 0.7 * jnp.sqrt(fraction / (1.0 - fraction))
    return jnp.sqrt(jnp.float32(0.1)) / sigma_level

def advantages(rewards, group_ids, kept_mask):
    choose = (group_ids[..., None] == jnp.arange(GROUPS, dtype=jnp.int32)).astype(jnp.float32)
    live_mask = choose * kept_mask[..., None]
    number = lax.optimization_barrier(jnp.sum(live_mask, axis=(0, 1)))
    reward_sum = lax.optimization_barrier(jnp.sum(live_mask * rewards[..., None], axis=(0, 1)))
    square = lax.optimization_barrier(jnp.sum(live_mask * (rewards * rewards)[..., None], axis=(0, 1)))
    group_mean = reward_sum / jnp.maximum(number, 1.0)
    spread = square / jnp.maximum(number, 1.0) - group_mean * group_mean
    centre = lax.optimization_barrier(jnp.sum(choose * group_mean, axis=-1))
    group_scale = lax.optimization_barrier(jnp.sum(choose * jnp.sqrt(jnp.maximum(spread, 1.0)), axis=-1))
    return (rewards - centre) / group_scale

def split_heads(matrix):
    return matrix.reshape(LEN, HEADS, HD).transpose(1, 0, 2)

def join_heads(stacked):
    return stacked.transpose(1, 0, 2).reshape(LEN, WIDTH)

def head_forward(q_head, k_head, v_head):
    scores = jnp.dot(q_head.astype(jnp.float32), k_head.astype(jnp.float32).T, precision=lax.Precision.HIGHEST) * HD ** (-0.5)
    row_max = lax.optimization_barrier(jnp.max(scores, axis=1, keepdims=True))
    weights = jnp.exp(scores - row_max)
    probabilities = (weights / lax.optimization_barrier(jnp.sum(weights, axis=1, keepdims=True))).astype(jnp.bfloat16)
    attended = jnp.dot(probabilities.astype(jnp.float32), v_head.astype(jnp.float32), precision=lax.Precision.HIGHEST).astype(jnp.bfloat16)
    return (probabilities, attended)

def head_backward(q_head, k_head, v_head, probabilities, attended, grad_attended):
    scale_factor = HD ** (-0.5)
    grad_full = grad_attended.astype(jnp.float32)
    row_dot = lax.optimization_barrier(jnp.sum(grad_full * attended.astype(jnp.float32), axis=1, keepdims=True))
    grad_probs = jnp.dot(grad_full, v_head.astype(jnp.float32).T, precision=lax.Precision.HIGHEST)
    prob_full = probabilities.astype(jnp.float32)
    grad_scores = (prob_full * (grad_probs - row_dot)).astype(jnp.bfloat16).astype(jnp.float32)
    grad_q = (jnp.dot(grad_scores, k_head.astype(jnp.float32), precision=lax.Precision.HIGHEST) * scale_factor).astype(jnp.bfloat16)
    grad_k = (jnp.dot(grad_scores.T, q_head.astype(jnp.float32), precision=lax.Precision.HIGHEST) * scale_factor).astype(jnp.bfloat16)
    grad_v = jnp.dot(prob_full.T, grad_full, precision=lax.Precision.HIGHEST).astype(jnp.bfloat16)
    return (grad_q, grad_k, grad_v)

def step_terms(query_in, key_in, value_in, sample_noise, old_velocity, gate_scale, coefficient, weight):
    heads_query = split_heads(query_in)
    heads_key = split_heads(key_in)
    heads_value = split_heads(value_in)
    probabilities, attended = lax.map(lambda head_items: head_forward(*head_items), (heads_query, heads_key, heads_value))
    mixed_rows = join_heads(attended).astype(jnp.float32)
    gate_full = gate_scale.astype(jnp.float32)[None, :]
    noise_rows = sample_noise.astype(jnp.float32)
    velocity_gap = gate_full * mixed_rows - old_velocity.astype(jnp.float32)
    misfit = jnp.sum(2.0 * coefficient * noise_rows * velocity_gap + coefficient * coefficient * velocity_gap * velocity_gap)
    log_full = -misfit / (2.0 * LEN * WIDTH)
    ratio_now = jnp.exp(log_full)
    grad_gap = weight * ratio_now * (coefficient * noise_rows + coefficient * coefficient * velocity_gap)
    grad_gate = lax.optimization_barrier(jnp.sum(grad_gap * mixed_rows, axis=0)).astype(jnp.bfloat16)
    grad_attended = (grad_gap * gate_full).astype(jnp.bfloat16)
    head_grads = lax.map(lambda head_items: head_backward(*head_items), (heads_query, heads_key, heads_value, probabilities, attended, split_heads(grad_attended)))
    return (join_heads(head_grads[0]), join_heads(head_grads[1]), join_heads(head_grads[2]), grad_gate, log_full.astype(jnp.bfloat16))

def skipped(operands):
    return (jnp.zeros((LEN, WIDTH), jnp.bfloat16), jnp.zeros((LEN, WIDTH), jnp.bfloat16), jnp.zeros((LEN, WIDTH), jnp.bfloat16), jnp.zeros((WIDTH,), jnp.bfloat16), jnp.zeros((), jnp.bfloat16))

def flatten(stacked):
    return stacked.reshape((SETS * STEPS,) + stacked.shape[2:])

def restore(stacked):
    return stacked.reshape((SETS, STEPS) + stacked.shape[1:])

def reference(query_in, key_in, value_in, sample_noise, old_velocity, gate_scale, rewards, group_ids, timesteps, counts):
    owner_rep = jnp.arange(STEPS, dtype=jnp.int32) // SLOTS
    slot_place = jnp.arange(STEPS, dtype=jnp.int32) % SLOTS
    kept_mask = (slot_place[None, :] < counts[:, owner_rep]).astype(jnp.float32)
    weight = kept_mask * advantages(rewards, group_ids, kept_mask)
    coefficient = step_coef(timesteps)

    def one_item(operands):
        return lax.cond(operands[-1] > 0.0, lambda inner: step_terms(*inner[:-1]), skipped, operands)
    results = lax.map(one_item, (flatten(query_in), flatten(key_in), flatten(value_in), flatten(sample_noise), flatten(old_velocity), flatten(gate_scale), flatten(coefficient), flatten(weight), flatten(kept_mask)))
    return (restore(results[0]), restore(results[1]), restore(results[2]), restore(results[3]), restore(results[4]))
```

```python
import functools

import jax
import jax.numpy as jnp
from jax import lax
from jax.experimental import pallas as pl
from jax.experimental.pallas import tpu as pltpu
from jax.sharding import PartitionSpec as P

HD = 128
GROUPS = 4
SIDE = 16
F32 = jnp.float32
BF16 = jnp.bfloat16
NN = (((1,), (0,)), ((), ()))
NT = (((1,), (1,)), ((), ()))
VMEM_LIMIT = 48 * 1024 * 1024


def step_coef(timesteps):
    fraction = timesteps.astype(F32) / 1000.0
    sigma_level = 0.7 * jnp.sqrt(fraction / (1.0 - fraction))
    return jnp.sqrt(jnp.float32(0.1)) / sigma_level


def dot(left, right, dims=NN):
    return lax.dot_general(left, right, dims, preferred_element_type=F32)


def fold_rows(values, reduce):
    rows, columns = values.shape
    return reduce(values.reshape(rows // 8, 8, columns), axis=0)


def pack_body(
    slot, coef_ref, query_ref, key_ref, value_ref, noise_ref, old_ref, out_ref, misfit_ref
):
    pieces = out_ref.shape[0]
    width = out_ref.shape[3]
    coefficient = coef_ref[slot]

    @pl.when(pl.program_id(0) == 0)
    def _():
        misfit_ref[...] = jnp.zeros_like(misfit_ref)

    total = misfit_ref[...]
    for piece in range(pieces):
        columns = slice(piece * width, (piece + 1) * width)
        out_ref[piece, 0] = query_ref[0, 0, :, columns]
        out_ref[piece, 1] = key_ref[0, 0, :, columns]
        out_ref[piece, 2] = value_ref[0, 0, :, columns]
        noise = noise_ref[0, 0, :, columns].astype(F32)
        shift = coefficient * old_ref[0, 0, :, columns].astype(F32)
        out_ref[piece, 3] = (noise - shift).astype(BF16)
        total = total + fold_rows(shift * (shift - 2.0 * noise), jnp.sum)
    misfit_ref[...] = total


def pack(slot, coefficient, arrays, groups):
    _, _, tokens, full_width = arrays[0].shape
    width = full_width // groups
    pieces = 4
    rows = pl.BlockSpec((1, 1, tokens, pieces * width), lambda i: (0, slot, 0, i))
    return pl.pallas_call(
        functools.partial(pack_body, slot),
        grid=(groups // pieces,),
        out_shape=(
            jax.ShapeDtypeStruct((groups, 4, tokens, width), BF16),
            jax.ShapeDtypeStruct((8, width), F32),
        ),
        in_specs=[pl.BlockSpec(memory_space=pltpu.SMEM)] + [rows] * 5,
        out_specs=(
            pl.BlockSpec((pieces, 4, tokens, width), lambda i: (i, 0, 0, 0)),
            pl.BlockSpec((8, width), lambda i: (0, 0)),
        ),
        compiler_params=pltpu.CompilerParams(vmem_limit_bytes=VMEM_LIMIT),
        cost_estimate=pl.CostEstimate(
            flops=6 * tokens * full_width,
            bytes_accessed=18 * tokens * full_width,
            transcendentals=0,
        ),
    )(coefficient, *arrays)


def attention_body(
    slot,
    block_rows,
    chunk,
    coef_ref,
    query_ref,
    key_ref,
    value_ref,
    field_ref,
    gate_ref,
    misfit_ref,
    out_ref,
    q_rows,
    k_rows,
    v_rows,
    k_cols,
    v_cols,
    field_cols,
    scores,
    weights,
    key_total,
    value_total,
    gate_total,
    misfit_total,
):
    length = q_rows.shape[0]
    pieces = out_ref.shape[0]
    tokens = length // pieces
    scale_factor = HD ** (-0.5)
    log2e = 1.4426950408889634
    coefficient = coef_ref[slot]
    q_rows[...] = query_ref[...].reshape(length, HD)
    k_rows[...] = key_ref[...].reshape(length, HD)
    v_rows[...] = value_ref[...].reshape(length, HD)
    k_cols[...] = k_rows[...].T
    v_cols[...] = v_rows[...].T
    field_cols[...] = field_ref[...].reshape(length, HD).T
    gate = gate_ref[...]
    gate_total[...] = jnp.zeros_like(gate_total)
    misfit_total[...] = jnp.zeros_like(misfit_total)
    chunks = [slice(at, at + chunk) for at in range(0, length, chunk)]

    def one_block(index, _):
        first = index == 0
        start = pl.multiple_of(index * block_rows, block_rows)
        rows_query = q_rows[pl.ds(start, block_rows), :]
        top = jnp.full((8, block_rows), -jnp.inf, F32)
        for part in chunks:
            block_scores = dot(k_rows[part, :], rows_query, NT)
            scores[part, :] = block_scores
            top = jnp.maximum(top, fold_rows(block_scores, jnp.max))
        row_max = jnp.max(top, axis=0, keepdims=True) * (scale_factor * log2e)
        sums = jnp.zeros((8, block_rows), F32)
        mixed = jnp.zeros((HD, block_rows), F32)
        for part in chunks:
            raised = jnp.exp2(scores[part, :] * (scale_factor * log2e) - row_max)
            sums = sums + fold_rows(raised, jnp.sum)
            rounded = raised.astype(BF16)
            weights[part, :] = rounded
            mixed = mixed + dot(v_cols[:, part], rounded)
        inverse = 1.0 / jnp.sum(sums, axis=0, keepdims=True)
        attended = (mixed * inverse).astype(BF16).astype(F32)
        field = field_cols[:, pl.ds(start, block_rows)].astype(F32)
        moved = coefficient * (gate * attended)
        misfit_total[...] += moved * (2.0 * field + moved)
        grad_gap = coefficient * (field + moved)
        gate_total[...] += grad_gap * attended
        grad_cols = (grad_gap * gate * inverse).astype(BF16)
        grad_rows = grad_cols.T
        row_dot = jnp.sum(grad_cols.astype(F32) * attended, axis=0, keepdims=True)
        grad_query = jnp.zeros((HD, block_rows), F32)
        for part in chunks:
            rounded = weights[part, :]
            grad_probs = dot(v_rows[part, :], grad_cols)
            grad_scores = (rounded.astype(F32) * (grad_probs - row_dot)).astype(BF16)
            grad_query = grad_query + dot(k_cols[:, part], grad_scores)
            value_part = dot(rounded, grad_rows)
            key_part = dot(grad_scores, rows_query)
            value_total[part, :] = jnp.where(first, value_part, value_total[part, :] + value_part)
            key_total[part, :] = jnp.where(first, key_part, key_total[part, :] + key_part)
        held = block_rows // tokens
        out_ref[pl.ds(index * held, held), 0:tokens, :] = (
            (grad_query.T * scale_factor).astype(BF16).reshape(held, tokens, HD)
        )
        return 0

    lax.fori_loop(0, length // block_rows, one_block, 0)
    out_ref[:, tokens : 2 * tokens, :] = (
        (key_total[...] * scale_factor).astype(BF16).reshape(pieces, tokens, HD)
    )
    out_ref[:, 2 * tokens : 3 * tokens, :] = (
        value_total[...].astype(BF16).reshape(pieces, tokens, HD)
    )

    def row_of(values):
        total = values[:, 0:HD]
        for at in range(HD, values.shape[1], HD):
            total = total + values[:, at : at + HD]
        return jnp.sum(total.T, axis=0, keepdims=True)

    gate_row = row_of(gate_total[...])
    misfit_row = row_of(misfit_total[...]) + jnp.sum(misfit_ref[...], axis=0, keepdims=True)
    rest = misfit_row
    side = []
    for _ in range(3):
        side.append(rest.astype(BF16).astype(F32))
        rest = rest - side[-1]
    gate_high = gate_row.astype(BF16).astype(F32)
    row_at = lax.broadcasted_iota(jnp.int32, (SIDE, HD), 0)
    rows = jnp.zeros((SIDE, HD), F32)
    for at, row in enumerate([gate_high, gate_row - gate_high] + side):
        rows = jnp.where(row_at == at, row, rows)
    out_ref[:, 3 * tokens :, :] = jnp.broadcast_to(
        rows.astype(BF16)[None], (pieces, SIDE, HD)
    )


def attention(slot, coefficient, arrived, gate_column, misfit):
    groups, _, tokens, width = arrived.shape
    length = groups * tokens
    heads_here = width // HD
    block_rows, chunk = 512, 512

    def field(which):
        return pl.BlockSpec((groups, 1, tokens, HD), lambda h: (0, which, 0, h))

    return pl.pallas_call(
        functools.partial(attention_body, slot, block_rows, chunk),
        grid=(heads_here,),
        out_shape=jax.ShapeDtypeStruct((groups, 3 * tokens + SIDE, width), BF16),
        in_specs=[pl.BlockSpec(memory_space=pltpu.SMEM)]
        + [field(which) for which in range(4)]
        + [
            pl.BlockSpec((HD, 1), lambda h: (h, 0)),
            pl.BlockSpec((8, HD), lambda h: (0, h)),
        ],
        out_specs=pl.BlockSpec((groups, 3 * tokens + SIDE, HD), lambda h: (0, 0, h)),
        scratch_shapes=[pltpu.VMEM((length, HD), BF16)] * 3
        + [pltpu.VMEM((HD, length), BF16)] * 3
        + [
            pltpu.VMEM((length, block_rows), F32),
            pltpu.VMEM((length, block_rows), BF16),
            pltpu.VMEM((length, HD), F32),
            pltpu.VMEM((length, HD), F32),
            pltpu.VMEM((HD, block_rows), F32),
            pltpu.VMEM((HD, block_rows), F32),
        ],
        compiler_params=pltpu.CompilerParams(vmem_limit_bytes=VMEM_LIMIT),
        cost_estimate=pl.CostEstimate(
            flops=heads_here * 24 * length * length * HD,
            bytes_accessed=14 * length * width,
            transcendentals=heads_here * length * length,
        ),
    )(coefficient, arrived, arrived, arrived, arrived, gate_column, misfit)


def unpack_body(slot, entries, weight_ref, main_ref, side_ref, *refs):
    query_ref, key_ref, value_ref, gate_ref, log_ref = refs[-5:]
    pieces = main_ref.shape[0]
    width = main_ref.shape[2]
    tokens = query_ref.shape[2]
    side = side_ref[...].astype(F32)
    misfit = jnp.sum(side[:, 2:5, :])
    ratio_log = jnp.full((1, HD), -misfit / (2.0 * entries), F32)
    log_ref[...] = jnp.broadcast_to(ratio_log, log_ref.shape)
    factor = weight_ref[slot] * jnp.exp(ratio_log)
    factor = jnp.concatenate([factor] * (width // HD), axis=1)
    gate_ref[...] = (side[:, 0, :] + side[:, 1, :]) * factor
    for piece in range(pieces):
        columns = slice(piece * width, (piece + 1) * width)
        for which, out_ref in enumerate((query_ref, key_ref, value_ref)):
            rows = main_ref[piece, which * tokens : (which + 1) * tokens, :].astype(F32)
            out_ref[0, 0, :, columns] = (rows * factor).astype(BF16)


def unpack(slot, slots, weight, returned, previous):
    groups, rows, width = returned.shape
    tokens = (rows - SIDE) // 3
    pieces = 4
    whole = jax.ShapeDtypeStruct((1, slots, tokens, groups * width), BF16)
    part = pl.BlockSpec((1, 1, tokens, pieces * width), lambda i: (0, slot, 0, i))
    held = [] if previous is None else list(previous)
    return pl.pallas_call(
        functools.partial(unpack_body, slot, groups * tokens * groups * width),
        grid=(groups // pieces,),
        out_shape=(
            whole,
            whole,
            whole,
            jax.ShapeDtypeStruct((groups, width), F32),
            jax.ShapeDtypeStruct((8, HD), F32),
        ),
        in_specs=[
            pl.BlockSpec(memory_space=pltpu.SMEM),
            pl.BlockSpec((pieces, 3 * tokens, width), lambda i: (i, 0, 0)),
            pl.BlockSpec((groups, SIDE, width), lambda i: (0, 3 * tokens // SIDE, 0)),
        ]
        + [pl.BlockSpec(memory_space=pl.ANY) for _ in held],
        out_specs=(
            part,
            part,
            part,
            pl.BlockSpec((groups, width), lambda i: (0, 0)),
            pl.BlockSpec((8, HD), lambda i: (0, 0)),
        ),
        input_output_aliases={3 + at: at for at in range(len(held))},
        compiler_params=pltpu.CompilerParams(vmem_limit_bytes=VMEM_LIMIT),
        cost_estimate=pl.CostEstimate(
            flops=3 * tokens * groups * width,
            bytes_accessed=12 * tokens * groups * width,
            transcendentals=0,
        ),
    )(weight, returned, returned, *held)


def exchange(pieces):
    return lax.all_to_all(pieces, "seq", split_axis=0, concat_axis=0, tiled=True)


def sum_over_replicas(values):
    replicas = lax.axis_size("rep")
    total = values
    for shift in range(1, replicas):
        total = total + lax.ppermute(
            values, "rep", [(at, (at + shift) % replicas) for at in range(replicas)]
        )
    return total


def local(
    query_in,
    key_in,
    value_in,
    sample_noise,
    old_velocity,
    gate_scale,
    rewards,
    group_ids,
    timesteps,
    counts,
):
    slots = query_in.shape[1]
    tokens = query_in.shape[2]
    full_width = query_in.shape[3]
    groups = lax.axis_size("seq")
    width = full_width // groups
    expert_at = lax.axis_index("expert")

    def own_expert(both):
        return lax.dynamic_index_in_dim(both, expert_at, 0, keepdims=False)

    coefficient = step_coef(own_expert(timesteps))
    arrays = (query_in, key_in, value_in, sample_noise, old_velocity)
    gate_here = lax.dynamic_slice_in_dim(
        gate_scale[0], lax.axis_index("seq") * width, width, 1
    ).astype(F32)

    kept_mask = (
        jnp.arange(slots, dtype=jnp.int32)[None, :] < counts[:, 0][:, None]
    ).astype(F32)
    choose = (group_ids[..., None] == jnp.arange(GROUPS, dtype=jnp.int32)).astype(F32)
    live_mask = choose * kept_mask[..., None]
    sums = sum_over_replicas(
        jnp.stack(
            (
                jnp.sum(live_mask, axis=(0, 1)),
                jnp.sum(live_mask * rewards[..., None], axis=(0, 1)),
                jnp.sum(live_mask * (rewards * rewards)[..., None], axis=(0, 1)),
            )
        )
    )
    number, reward_sum, square = sums[0], sums[1], sums[2]
    group_mean = reward_sum / jnp.maximum(number, 1.0)
    spread = square / jnp.maximum(number, 1.0) - group_mean * group_mean
    centre = jnp.sum(choose * group_mean, axis=-1)
    group_scale = jnp.sum(choose * jnp.sqrt(jnp.maximum(spread, 1.0)), axis=-1)
    advantage = (rewards - centre) / group_scale
    kept_here = own_expert(kept_mask)
    weight = own_expert(kept_mask * advantage)

    arrived, misfits = [], []
    for slot in range(slots):
        packed, misfit = pack(slot, coefficient, arrays, groups)
        arrived.append(
            exchange(packed.reshape(groups, 4 * tokens, width)).reshape(packed.shape)
        )
        misfits.append(misfit)
    returned = []
    for slot in range(slots):
        returned.append(
            exchange(
                attention(
                    slot, coefficient, arrived[slot], gate_here[slot][:, None], misfits[slot]
                )
            )
        )
    held = None
    gates, logs = [], []
    for slot in range(slots):
        *held, gate_rows, log_rows = unpack(slot, slots, weight, returned[slot], held)
        gates.append(gate_rows.reshape(full_width).astype(BF16))
        logs.append((log_rows[0, 0] * kept_here[slot]).astype(BF16))
    return (
        held[0],
        held[1],
        held[2],
        jnp.stack(gates)[None],
        jnp.stack(logs)[None],
    )


def solution(mesh):
    placed = (
        P("expert", "rep", "seq", None),
        P("expert", "rep", "seq", None),
        P("expert", "rep", "seq", None),
        P("expert", "rep", "seq", None),
        P("expert", "rep", "seq", None),
        P("expert", "rep", None),
        P(None, "rep"),
        P(None, "rep"),
        P(None, "rep"),
        P(None, "rep"),
    )
    return jax.shard_map(
        local,
        mesh=mesh,
        in_specs=placed,
        out_specs=(
            P("expert", "rep", "seq", None),
            P("expert", "rep", "seq", None),
            P("expert", "rep", "seq", None),
            P("expert", "rep", None),
            P("expert", "rep"),
        ),
        check_vma=False,
    )
```

```python
import functools

import jax
import jax.numpy as jnp
from jax import lax
from jax.experimental import pallas as pl
from jax.experimental.pallas import tpu as pltpu
from jax.sharding import PartitionSpec as P

HD = 128
GROUPS = 4
SIDE = 16
F32 = jnp.float32
BF16 = jnp.bfloat16
NN = (((1,), (0,)), ((), ()))
NT = (((1,), (1,)), ((), ()))
VMEM_LIMIT = 63 * 1024 * 1024


def step_coef(timesteps):
    fraction = timesteps.astype(F32) / 1000.0
    sigma_level = 0.7 * jnp.sqrt(fraction / (1.0 - fraction))
    return jnp.sqrt(jnp.float32(0.1)) / sigma_level


def dot(left, right, dims=NN):
    return lax.dot_general(left, right, dims, preferred_element_type=F32)


def fold_rows(values, reduce):
    rows, columns = values.shape
    return reduce(values.reshape(rows // 8, 8, columns), axis=0)


def pack_body(
    slot, own_ref, coef_ref, query_ref, key_ref, value_ref, noise_ref, old_ref, *refs
):
    out_ref, misfit_ref = refs[-2:]
    pieces, _, width = out_ref.shape
    tokens = query_ref.shape[2]
    coefficient = coef_ref[own_ref[0], slot]

    @pl.when(pl.program_id(0) == 0)
    def _():
        misfit_ref[...] = jnp.zeros_like(misfit_ref)

    total = misfit_ref[...]
    for piece in range(pieces):
        columns = slice(piece * width, (piece + 1) * width)
        out_ref[piece, 0:tokens] = query_ref[0, 0, :, columns]
        out_ref[piece, tokens : 2 * tokens] = key_ref[0, 0, :, columns]
        out_ref[piece, 2 * tokens : 3 * tokens] = value_ref[0, 0, :, columns]
        noise = noise_ref[0, 0, :, columns].astype(F32)
        shift = coefficient * old_ref[0, 0, :, columns].astype(F32)
        out_ref[piece, 3 * tokens : 4 * tokens] = (noise - shift).astype(BF16)
        total = total + fold_rows(shift * (shift - 2.0 * noise), jnp.sum)
        for gate_ref in refs[:-2]:
            gates = gate_ref[0, :, columns]
            blank = jnp.zeros((SIDE - gates.shape[0], width), BF16)
            out_ref[piece, 4 * tokens :] = jnp.concatenate([gates, blank], axis=0)
    misfit_ref[...] = total


def pack(slot, own, coefficient, arrays, gate_scale, groups):
    _, _, tokens, full_width = arrays[0].shape
    width = full_width // groups
    pieces = 8
    rows = pl.BlockSpec((1, 1, tokens, pieces * width), lambda i: (0, slot, 0, i))
    gates = [] if gate_scale is None else [gate_scale]
    held = 4 * tokens + SIDE * len(gates)
    return pl.pallas_call(
        functools.partial(pack_body, slot),
        grid=(groups // pieces,),
        out_shape=(
            jax.ShapeDtypeStruct((groups, held, width), BF16),
            jax.ShapeDtypeStruct((8, width), F32),
        ),
        in_specs=[pl.BlockSpec(memory_space=pltpu.SMEM)] * 2
        + [rows] * 5
        + [pl.BlockSpec((1,) + g.shape[1:2] + (pieces * width,), lambda i: (0, 0, i)) for g in gates],
        out_specs=(
            pl.BlockSpec((pieces, held, width), lambda i: (i, 0, 0)),
            pl.BlockSpec((8, width), lambda i: (0, 0)),
        ),
        compiler_params=pltpu.CompilerParams(vmem_limit_bytes=VMEM_LIMIT),
        cost_estimate=pl.CostEstimate(
            flops=6 * tokens * full_width,
            bytes_accessed=18 * tokens * full_width,
            transcendentals=0,
        ),
    )(own, coefficient, *arrays, *gates)


def attention_body(
    slot,
    block_rows,
    chunk,
    own_ref,
    coef_ref,
    query_ref,
    key_ref,
    value_ref,
    field_ref,
    gate_ref,
    misfit_ref,
    out_ref,
    q_rows,
    k_rows,
    v_rows,
    k_cols,
    v_cols,
    field_cols,
    scores,
    weights,
    key_total,
    value_total,
    gate_total,
    misfit_total,
):
    length = q_rows.shape[0]
    pieces = out_ref.shape[1]
    tokens = length // pieces
    step_set = pl.program_id(0)
    scale_factor = HD ** (-0.5)
    log2e = 1.4426950408889634
    coefficient = coef_ref[step_set, slot]
    q_rows[...] = query_ref[...].reshape(length, HD)
    k_rows[...] = key_ref[...].reshape(length, HD)
    v_rows[...] = value_ref[...].reshape(length, HD)
    k_cols[...] = k_rows[...].T
    v_cols[...] = v_rows[...].T
    field_cols[...] = field_ref[...].reshape(length, HD).T
    gate_row = gate_ref[0, 0, slot : slot + 1, :].astype(F32)
    gate = jnp.broadcast_to(gate_row, (8, HD)).T[:, 0:1]
    gate_total[...] = jnp.zeros_like(gate_total)
    misfit_total[...] = jnp.zeros_like(misfit_total)
    chunks = [slice(at, at + chunk) for at in range(0, length, chunk)]

    def one_block(index, _):
        first = index == 0
        start = pl.multiple_of(index * block_rows, block_rows)
        rows_query = q_rows[pl.ds(start, block_rows), :]
        top = jnp.full((8, block_rows), -jnp.inf, F32)
        for part in chunks:
            block_scores = dot(k_rows[part, :], rows_query, NT)
            scores[part, :] = block_scores
            top = jnp.maximum(top, fold_rows(block_scores, jnp.max))
        row_max = jnp.max(top, axis=0, keepdims=True) * (scale_factor * log2e)
        sums = jnp.zeros((8, block_rows), F32)
        mixed = jnp.zeros((HD, block_rows), F32)
        for part in chunks:
            raised = jnp.exp2(scores[part, :] * (scale_factor * log2e) - row_max)
            sums = sums + fold_rows(raised, jnp.sum)
            rounded = raised.astype(BF16)
            weights[part, :] = rounded
            mixed = mixed + dot(v_cols[:, part], rounded)
        inverse = 1.0 / jnp.sum(sums, axis=0, keepdims=True)
        attended = (mixed * inverse).astype(BF16).astype(F32)
        field = field_cols[:, pl.ds(start, block_rows)].astype(F32)
        moved = coefficient * (gate * attended)
        misfit_total[...] += moved * (2.0 * field + moved)
        grad_gap = coefficient * (field + moved)
        gate_total[...] += grad_gap * attended
        grad_cols = (grad_gap * gate * inverse).astype(BF16)
        grad_rows = grad_cols.T
        row_dot = jnp.sum(grad_cols.astype(F32) * attended, axis=0, keepdims=True)
        grad_query = jnp.zeros((HD, block_rows), F32)
        for part in chunks:
            rounded = weights[part, :]
            grad_probs = dot(v_rows[part, :], grad_cols)
            grad_scores = (rounded.astype(F32) * (grad_probs - row_dot)).astype(BF16)
            grad_query = grad_query + dot(k_cols[:, part], grad_scores)
            value_part = dot(rounded, grad_rows)
            key_part = dot(grad_scores, rows_query)
            value_total[part, :] = jnp.where(first, value_part, value_total[part, :] + value_part)
            key_total[part, :] = jnp.where(first, key_part, key_total[part, :] + key_part)
        held = block_rows // tokens
        out_ref[0, pl.ds(index * held, held), 0:tokens, :] = (
            (grad_query.T * scale_factor).astype(BF16).reshape(held, tokens, HD)
        )
        return 0

    lax.fori_loop(0, length // block_rows, one_block, 0)
    out_ref[0, :, tokens : 2 * tokens, :] = (
        (key_total[...] * scale_factor).astype(BF16).reshape(pieces, tokens, HD)
    )
    out_ref[0, :, 2 * tokens : 3 * tokens, :] = (
        value_total[...].astype(BF16).reshape(pieces, tokens, HD)
    )

    def row_of(values):
        total = values[:, 0:HD]
        for at in range(HD, values.shape[1], HD):
            total = total + values[:, at : at + HD]
        return jnp.sum(total.T, axis=0, keepdims=True)

    gate_row = row_of(gate_total[...])
    local_row = jnp.sum(misfit_ref[...], axis=0, keepdims=True)
    misfit_row = row_of(misfit_total[...]) + jnp.where(step_set == own_ref[0], local_row, 0.0)
    rest = misfit_row
    side = []
    for _ in range(3):
        side.append(rest.astype(BF16).astype(F32))
        rest = rest - side[-1]
    gate_high = gate_row.astype(BF16).astype(F32)
    row_at = lax.broadcasted_iota(jnp.int32, (SIDE, HD), 0)
    rows = jnp.zeros((SIDE, HD), F32)
    for at, row in enumerate([gate_high, gate_row - gate_high] + side):
        rows = jnp.where(row_at == at, row, rows)
    out_ref[0, :, 3 * tokens :, :] = jnp.broadcast_to(
        rows.astype(BF16)[None], (pieces, SIDE, HD)
    )


def attention(slot, own, coefficient, arrived, gates, misfit):
    sets, groups, _, width = arrived.shape
    tokens = arrived.shape[2] // (4 * SIDE) * SIDE
    length = groups * tokens
    block_rows, chunk = 512, 512

    def field(which):
        return pl.BlockSpec((1, groups, tokens, HD), lambda e: (e, 0, which, 0))

    return pl.pallas_call(
        functools.partial(attention_body, slot, block_rows, chunk),
        grid=(sets,),
        out_shape=jax.ShapeDtypeStruct((sets, groups, 3 * tokens + SIDE, width), BF16),
        in_specs=[pl.BlockSpec(memory_space=pltpu.SMEM)] * 2
        + [field(which) for which in range(4)]
        + [
            pl.BlockSpec((1, 1, SIDE, HD), lambda e: (e, 0, 4 * tokens // SIDE, 0)),
            pl.BlockSpec((8, HD), lambda e: (0, 0)),
        ],
        out_specs=pl.BlockSpec((1, groups, 3 * tokens + SIDE, HD), lambda e: (e, 0, 0, 0)),
        scratch_shapes=[pltpu.VMEM((length, HD), BF16)] * 3
        + [pltpu.VMEM((HD, length), BF16)] * 3
        + [
            pltpu.VMEM((length, block_rows), F32),
            pltpu.VMEM((length, block_rows), BF16),
            pltpu.VMEM((length, HD), F32),
            pltpu.VMEM((length, HD), F32),
            pltpu.VMEM((HD, block_rows), F32),
            pltpu.VMEM((HD, block_rows), F32),
        ],
        compiler_params=pltpu.CompilerParams(vmem_limit_bytes=VMEM_LIMIT),
        cost_estimate=pl.CostEstimate(
            flops=sets * 24 * length * length * HD,
            bytes_accessed=sets * 14 * length * width,
            transcendentals=sets * length * length,
        ),
    )(own, coefficient, arrived, arrived, arrived, arrived, gates, misfit)


def unpack_body(slot, entries, weight_ref, kept_ref, main_ref, side_ref, *refs):
    query_ref, key_ref, value_ref, gate_ref, log_ref = refs[-5:]
    earlier = refs[:-5]
    pieces = main_ref.shape[0]
    width = main_ref.shape[2]
    tokens = query_ref.shape[2]
    misfit = jnp.sum(side_ref[:, 2:5, :].astype(F32))
    ratio_log = jnp.full((1, HD), -misfit / (2.0 * entries), F32)
    if earlier:
        gate_ref[0, 0:1, :] = earlier[0][...].astype(BF16)
        own_log = ratio_log[:, 0:1] * kept_ref[slot]
        log_ref[...] = jnp.concatenate([earlier[1][:, 0:1], own_log], axis=1).astype(BF16)
    else:
        log_ref[...] = ratio_log * kept_ref[slot]
    factor = weight_ref[slot] * jnp.exp(ratio_log)
    first = pl.program_id(0) * pieces
    for piece in range(pieces):
        columns = slice(piece * width, (piece + 1) * width)
        parts = side_ref[first + piece, 0:2, :].astype(F32)
        gate_row = (parts[0:1] + parts[1:2]) * factor
        if earlier:
            gate_ref[0, 1:2, columns] = gate_row.astype(BF16)
        else:
            gate_ref[:, columns] = gate_row
        for which, out_ref in enumerate((query_ref, key_ref, value_ref)):
            rows = main_ref[piece, which * tokens : (which + 1) * tokens, :].astype(F32)
            out_ref[0, 0, :, columns] = (rows * factor).astype(BF16)


def unpack(slot, slots, weight, kept, returned, previous):
    heads, rows, width = returned.shape
    tokens = (rows - SIDE) // 3
    full_width = heads * width
    entries = full_width * tokens * lax.axis_size("seq")
    pieces = 8
    whole = jax.ShapeDtypeStruct((1, slots, tokens, full_width), BF16)
    part = pl.BlockSpec((1, 1, tokens, pieces * width), lambda i: (0, slot, 0, i))
    in_specs = [
        pl.BlockSpec(memory_space=pltpu.SMEM),
        pl.BlockSpec(memory_space=pltpu.SMEM),
        pl.BlockSpec((pieces, 3 * tokens, width), lambda i: (i, 0, 0)),
        pl.BlockSpec((heads, SIDE, width), lambda i: (0, 3 * tokens // SIDE, 0)),
    ]
    if previous:
        in_specs += [pl.BlockSpec(memory_space=pl.ANY)] * 3 + [
            pl.BlockSpec((1, pieces * width), lambda i: (0, i)),
            pl.BlockSpec((1, HD), lambda i: (0, 0)),
        ]
        small = (
            jax.ShapeDtypeStruct((1, slots, full_width), BF16),
            jax.ShapeDtypeStruct((1, slots), BF16),
        )
        small_specs = (
            pl.BlockSpec((1, slots, pieces * width), lambda i: (0, 0, i)),
            pl.BlockSpec((1, slots), lambda i: (0, 0)),
        )
    else:
        small = (
            jax.ShapeDtypeStruct((1, full_width), F32),
            jax.ShapeDtypeStruct((1, HD), F32),
        )
        small_specs = (
            pl.BlockSpec((1, pieces * width), lambda i: (0, i)),
            pl.BlockSpec((1, HD), lambda i: (0, 0)),
        )

    def body(weight_ref, kept_ref, main_ref, side_ref, *refs):
        refs = refs[3:] if previous else refs
        unpack_body(slot, entries, weight_ref, kept_ref, main_ref, side_ref, *refs)

    return pl.pallas_call(
        body,
        grid=(heads // pieces,),
        out_shape=(whole, whole, whole) + small,
        in_specs=in_specs,
        out_specs=(part, part, part) + small_specs,
        input_output_aliases={4 + at: at for at in range(3)} if previous else {},
        compiler_params=pltpu.CompilerParams(vmem_limit_bytes=VMEM_LIMIT),
        cost_estimate=pl.CostEstimate(
            flops=3 * tokens * full_width,
            bytes_accessed=12 * tokens * full_width,
            transcendentals=0,
        ),
    )(weight, kept, returned, returned, *previous)


def exchange(pieces):
    return lax.all_to_all(pieces, ("expert", "seq"), split_axis=0, concat_axis=0, tiled=True)


def sum_over_replicas(values):
    replicas = lax.axis_size("rep")
    total = values
    for shift in range(1, replicas):
        total = total + lax.ppermute(
            values, "rep", [(at, (at + shift) % replicas) for at in range(replicas)]
        )
    return total


def local(
    query_in,
    key_in,
    value_in,
    sample_noise,
    old_velocity,
    gate_scale,
    rewards,
    group_ids,
    timesteps,
    counts,
):
    slots = query_in.shape[1]
    tokens = query_in.shape[2]
    full_width = query_in.shape[3]
    groups = lax.axis_size("seq")
    sets = lax.axis_size("expert")
    heads = sets * groups
    width = full_width // heads
    expert_at = lax.axis_index("expert")
    own = expert_at.astype(jnp.int32)[None]

    def own_expert(both):
        return lax.dynamic_index_in_dim(both, expert_at, 0, keepdims=False)

    coefficient = step_coef(timesteps)
    arrays = (query_in, key_in, value_in, sample_noise, old_velocity)
    kept_mask = (
        jnp.arange(slots, dtype=jnp.int32)[None, :] < counts[:, 0][:, None]
    ).astype(F32)
    choose = (group_ids[..., None] == jnp.arange(GROUPS, dtype=jnp.int32)).astype(F32)
    live_mask = choose * kept_mask[..., None]
    sums = sum_over_replicas(
        jnp.stack(
            (
                jnp.sum(live_mask, axis=(0, 1)),
                jnp.sum(live_mask * rewards[..., None], axis=(0, 1)),
                jnp.sum(live_mask * (rewards * rewards)[..., None], axis=(0, 1)),
            )
        )
    )
    number, reward_sum, square = sums[0], sums[1], sums[2]
    group_mean = reward_sum / jnp.maximum(number, 1.0)
    spread = square / jnp.maximum(number, 1.0) - group_mean * group_mean
    centre = jnp.sum(choose * group_mean, axis=-1)
    group_scale = jnp.sum(choose * jnp.sqrt(jnp.maximum(spread, 1.0)), axis=-1)
    advantage = (rewards - centre) / group_scale
    kept_here = own_expert(kept_mask)
    weight = own_expert(kept_mask * advantage)

    arrived, misfits = [], []
    for slot in range(slots):
        packed, misfit = pack(
            slot, own, coefficient, arrays, gate_scale if slot == 0 else None, heads
        )
        arrived.append(exchange(packed).reshape((sets, groups) + packed.shape[1:]))
        misfits.append(misfit)
    returned = []
    for slot in range(slots):
        sent = attention(
            slot, own, coefficient, arrived[slot], arrived[0], misfits[slot]
        )
        returned.append(exchange(sent.reshape(heads, 3 * tokens + SIDE, width)))
    held = ()
    for slot in range(slots):
        held = unpack(slot, slots, weight, kept_here, returned[slot], held)
    return held


def solution(mesh):
    placed = (
        P("expert", "rep", "seq", None),
        P("expert", "rep", "seq", None),
        P("expert", "rep", "seq", None),
        P("expert", "rep", "seq", None),
        P("expert", "rep", "seq", None),
        P("expert", "rep", None),
        P(None, "rep"),
        P(None, "rep"),
        P(None, "rep"),
        P(None, "rep"),
    )
    return jax.shard_map(
        local,
        mesh=mesh,
        in_specs=placed,
        out_specs=(
            P("expert", "rep", "seq", None),
            P("expert", "rep", "seq", None),
            P("expert", "rep", "seq", None),
            P("expert", "rep", None),
            P("expert", "rep"),
        ),
        check_vma=False,
    )
```

```python
import functools

import jax
import jax.numpy as jnp
from jax import lax
from jax.experimental import pallas as pl
from jax.experimental.pallas import tpu as pltpu
from jax.sharding import PartitionSpec as P

HD = 128
GROUPS = 4
GATE_ROWS = 16
SIDE = 16
F32 = jnp.float32
BF16 = jnp.bfloat16
NN = (((1,), (0,)), ((), ()))
NT = (((1,), (1,)), ((), ()))
VMEM_LIMIT = 63 * 1024 * 1024


def step_coef(timestep, shape):
    fraction = jnp.full(shape, timestep.astype(F32)) / 1000.0
    sigma_level = 0.7 * jnp.sqrt(fraction / (1.0 - fraction))
    return jnp.sqrt(jnp.float32(0.1)) / sigma_level


def dot(left, right, dims=NN):
    return lax.dot_general(left, right, dims, preferred_element_type=F32)


def fold_rows(values, reduce):
    rows, columns = values.shape
    return reduce(values.reshape(rows // 8, 8, columns), axis=0)


def pack_body(
    slot, steps_ref, query_ref, key_ref, value_ref, noise_ref, old_ref, *refs
):
    out_ref, misfit_ref = refs[-2:]
    pieces, _, width = out_ref.shape
    tokens = query_ref.shape[2]
    coefficient = step_coef(steps_ref[lax.axis_index("expert"), slot], (8, width))[0:1]

    @pl.when(pl.program_id(0) == 0)
    def _():
        misfit_ref[...] = jnp.zeros_like(misfit_ref)

    total = misfit_ref[...]
    for piece in range(pieces):
        columns = slice(piece * width, (piece + 1) * width)
        out_ref[piece, 0:tokens] = query_ref[0, 0, :, columns]
        out_ref[piece, tokens : 2 * tokens] = key_ref[0, 0, :, columns]
        out_ref[piece, 2 * tokens : 3 * tokens] = value_ref[0, 0, :, columns]
        noise = noise_ref[0, 0, :, columns].astype(F32)
        shift = coefficient * old_ref[0, 0, :, columns].astype(F32)
        out_ref[piece, 3 * tokens : 4 * tokens] = (noise - shift).astype(BF16)
        total = total + fold_rows(shift * (shift - 2.0 * noise), jnp.sum)
        for gate_ref in refs[:-2]:
            gates = gate_ref[0, :, columns]
            blank = jnp.zeros((GATE_ROWS - gates.shape[0], width), BF16)
            out_ref[piece, 4 * tokens :] = jnp.concatenate([gates, blank], axis=0)
    misfit_ref[...] = total


def pack(slot, timesteps, arrays, gate_scale, groups):
    _, _, tokens, full_width = arrays[0].shape
    width = full_width // groups
    pieces = 16
    rows = pl.BlockSpec((1, 1, tokens, pieces * width), lambda i: (0, slot, 0, i))
    gates = [] if gate_scale is None else [gate_scale]
    held = 4 * tokens + GATE_ROWS * len(gates)
    return pl.pallas_call(
        functools.partial(pack_body, slot),
        grid=(groups // pieces,),
        out_shape=(
            jax.ShapeDtypeStruct((groups, held, width), BF16),
            jax.ShapeDtypeStruct((8, width), F32),
        ),
        in_specs=[pl.BlockSpec(memory_space=pltpu.SMEM)]
        + [rows] * 5
        + [pl.BlockSpec((1,) + g.shape[1:2] + (pieces * width,), lambda i: (0, 0, i)) for g in gates],
        out_specs=(
            pl.BlockSpec((pieces, held, width), lambda i: (i, 0, 0)),
            pl.BlockSpec((8, width), lambda i: (0, 0)),
        ),
        compiler_params=pltpu.CompilerParams(vmem_limit_bytes=VMEM_LIMIT),
        cost_estimate=pl.CostEstimate(
            flops=6 * tokens * full_width,
            bytes_accessed=18 * tokens * full_width,
            transcendentals=0,
        ),
    )(timesteps, *arrays, *gates)


def attention_body(
    slot,
    block_rows,
    chunk,
    steps_ref,
    query_ref,
    key_ref,
    value_ref,
    field_ref,
    gate_ref,
    misfit_ref,
    out_ref,
    q_rows,
    k_rows,
    v_rows,
    k_cols,
    v_cols,
    field_cols,
    scores,
    weights,
    key_total,
    value_total,
    gate_total,
    misfit_total,
):
    length = q_rows.shape[0]
    pieces = out_ref.shape[1]
    tokens = length // pieces
    step_set = pl.program_id(0)
    scale_factor = HD ** (-0.5)
    log2e = 1.4426950408889634
    coefficient = step_coef(steps_ref[step_set, slot], (8, block_rows))[0:1]
    q_rows[...] = query_ref[...].reshape(length, HD)
    k_rows[...] = key_ref[...].reshape(length, HD)
    v_rows[...] = value_ref[...].reshape(length, HD)
    k_cols[...] = k_rows[...].T
    v_cols[...] = v_rows[...].T
    field_cols[...] = field_ref[...].reshape(length, HD).T
    gate_row = gate_ref[0, 0, slot : slot + 1, :].astype(F32)
    gate = jnp.broadcast_to(gate_row, (8, HD)).T[:, 0:1]
    gate_total[...] = jnp.zeros_like(gate_total)
    misfit_total[...] = jnp.zeros_like(misfit_total)
    chunks = [slice(at, at + chunk) for at in range(0, length, chunk)]

    def one_block(index, _):
        first = index == 0
        start = pl.multiple_of(index * block_rows, block_rows)
        rows_query = q_rows[pl.ds(start, block_rows), :]
        top = jnp.full((8, block_rows), -jnp.inf, F32)
        for part in chunks:
            block_scores = dot(k_rows[part, :], rows_query, NT)
            scores[part, :] = block_scores
            top = jnp.maximum(top, fold_rows(block_scores, jnp.max))
        row_max = jnp.max(top, axis=0, keepdims=True)
        sums = jnp.zeros((8, block_rows), F32)
        mixed = jnp.zeros((HD, block_rows), F32)
        for part in chunks:
            raised = jnp.exp2((scores[part, :] - row_max) * (scale_factor * log2e))
            sums = sums + fold_rows(raised, jnp.sum)
            rounded = raised.astype(BF16)
            weights[part, :] = rounded
            mixed = mixed + dot(v_cols[:, part], rounded)
        inverse = 1.0 / jnp.sum(sums, axis=0, keepdims=True)
        attended = (mixed * inverse).astype(BF16).astype(F32)
        field = field_cols[:, pl.ds(start, block_rows)].astype(F32)
        moved = coefficient * (gate * attended)
        misfit_total[...] += moved * (2.0 * field + moved)
        grad_gap = coefficient * (field + moved)
        gate_total[...] += grad_gap * attended
        grad_cols = (grad_gap * gate * inverse).astype(BF16)
        grad_rows = grad_cols.T
        row_dot = jnp.sum(grad_cols.astype(F32) * attended, axis=0, keepdims=True)
        grad_query = jnp.zeros((HD, block_rows), F32)
        for part in chunks:
            rounded = weights[part, :]
            grad_probs = dot(v_rows[part, :], grad_cols)
            grad_scores = (rounded.astype(F32) * (grad_probs - row_dot)).astype(BF16)
            grad_query = grad_query + dot(k_cols[:, part], grad_scores)
            value_part = dot(rounded, grad_rows)
            key_part = dot(grad_scores, rows_query)
            value_total[part, :] = jnp.where(first, value_part, value_total[part, :] + value_part)
            key_total[part, :] = jnp.where(first, key_part, key_total[part, :] + key_part)
        held = block_rows // tokens
        out_ref[0, pl.ds(index * held, held), 0:tokens, :] = (
            (grad_query.T * scale_factor).astype(BF16).reshape(held, tokens, HD)
        )
        return 0

    lax.fori_loop(0, length // block_rows, one_block, 0)
    out_ref[0, :, tokens : 2 * tokens, :] = (
        (key_total[...] * scale_factor).astype(BF16).reshape(pieces, tokens, HD)
    )
    out_ref[0, :, 2 * tokens : 3 * tokens, :] = (
        value_total[...].astype(BF16).reshape(pieces, tokens, HD)
    )

    def row_of(values):
        total = values[:, 0:HD]
        for at in range(HD, values.shape[1], HD):
            total = total + values[:, at : at + HD]
        return jnp.sum(total.T, axis=0, keepdims=True)

    gate_row = row_of(gate_total[...])
    local_row = jnp.sum(misfit_ref[...], axis=0, keepdims=True)
    misfit_row = row_of(misfit_total[...]) + jnp.where(step_set == lax.axis_index("expert"), local_row, 0.0)
    rest = misfit_row
    side = []
    for _ in range(3):
        side.append(rest.astype(BF16).astype(F32))
        rest = rest - side[-1]
    gate_high = gate_row.astype(BF16).astype(F32)
    row_at = lax.broadcasted_iota(jnp.int32, (SIDE, HD), 0)
    rows = jnp.zeros((SIDE, HD), F32)
    for at, row in enumerate([gate_high, gate_row - gate_high] + side):
        rows = jnp.where(row_at == at, row, rows)
    out_ref[0, :, 3 * tokens :, :] = jnp.broadcast_to(
        rows.astype(BF16)[None], (pieces, SIDE, HD)
    )


def attention(slot, timesteps, arrived, gates, misfit):
    sets, groups, _, width = arrived.shape
    tokens = arrived.shape[2] // (4 * GATE_ROWS) * GATE_ROWS
    length = groups * tokens
    block_rows, chunk = 512, 512

    def field(which):
        return pl.BlockSpec((1, groups, tokens, HD), lambda e: (e, 0, which, 0))

    return pl.pallas_call(
        functools.partial(attention_body, slot, block_rows, chunk),
        grid=(sets,),
        out_shape=jax.ShapeDtypeStruct((sets, groups, 3 * tokens + SIDE, width), BF16),
        in_specs=[pl.BlockSpec(memory_space=pltpu.SMEM)]
        + [field(which) for which in range(4)]
        + [
            pl.BlockSpec((1, 1, GATE_ROWS, HD), lambda e: (e, 0, 4 * tokens // GATE_ROWS, 0)),
            pl.BlockSpec((8, HD), lambda e: (0, 0)),
        ],
        out_specs=pl.BlockSpec((1, groups, 3 * tokens + SIDE, HD), lambda e: (e, 0, 0, 0)),
        scratch_shapes=[pltpu.VMEM((length, HD), BF16)] * 3
        + [pltpu.VMEM((HD, length), BF16)] * 3
        + [
            pltpu.VMEM((length, block_rows), F32),
            pltpu.VMEM((length, block_rows), BF16),
            pltpu.VMEM((length, HD), F32),
            pltpu.VMEM((length, HD), F32),
            pltpu.VMEM((HD, block_rows), F32),
            pltpu.VMEM((HD, block_rows), F32),
        ],
        compiler_params=pltpu.CompilerParams(vmem_limit_bytes=VMEM_LIMIT),
        cost_estimate=pl.CostEstimate(
            flops=sets * 24 * length * length * HD,
            bytes_accessed=sets * 14 * length * width,
            transcendentals=sets * length * length,
        ),
    )(timesteps, arrived, arrived, arrived, arrived, gates, misfit)


def unpack_body(slot, entries, weight_ref, kept_ref, main_ref, side_ref, *refs):
    query_ref, key_ref, value_ref, gate_ref, log_ref = refs[-5:]
    earlier = refs[:-5]
    pieces = main_ref.shape[0]
    width = main_ref.shape[2]
    tokens = query_ref.shape[2]
    misfit = jnp.sum(side_ref[:, 2:5, :].astype(F32))
    ratio_log = jnp.full((1, HD), -misfit / (2.0 * entries), F32)
    if earlier:
        gate_ref[0, 0:1, :] = earlier[0][...].astype(BF16)
        own_log = ratio_log[:, 0:1] * kept_ref[slot]
        log_ref[...] = jnp.concatenate([earlier[1][:, 0:1], own_log], axis=1).astype(BF16)
    else:
        log_ref[...] = ratio_log * kept_ref[slot]
    factor = weight_ref[slot] * jnp.exp(ratio_log)
    first = pl.program_id(0) * pieces
    for piece in range(pieces):
        columns = slice(piece * width, (piece + 1) * width)
        parts = side_ref[first + piece, 0:2, :].astype(F32)
        gate_row = (parts[0:1] + parts[1:2]) * factor
        if earlier:
            gate_ref[0, 1:2, columns] = gate_row.astype(BF16)
        else:
            gate_ref[:, columns] = gate_row
        for which, out_ref in enumerate((query_ref, key_ref, value_ref)):
            rows = main_ref[piece, which * tokens : (which + 1) * tokens, :].astype(F32)
            out_ref[0, 0, :, columns] = (rows * factor).astype(BF16)


def unpack(slot, slots, weight, kept, returned, previous):
    heads, rows, width = returned.shape
    tokens = (rows - SIDE) // 3
    full_width = heads * width
    entries = full_width * tokens * lax.axis_size("seq")
    pieces = 16
    whole = jax.ShapeDtypeStruct((1, slots, tokens, full_width), BF16)
    part = pl.BlockSpec((1, 1, tokens, pieces * width), lambda i: (0, slot, 0, i))
    in_specs = [
        pl.BlockSpec(memory_space=pltpu.SMEM),
        pl.BlockSpec(memory_space=pltpu.SMEM),
        pl.BlockSpec((pieces, 3 * tokens, width), lambda i: (i, 0, 0)),
        pl.BlockSpec((heads, SIDE, width), lambda i: (0, 3 * tokens // SIDE, 0)),
    ]
    if previous:
        in_specs += [pl.BlockSpec(memory_space=pl.ANY)] * 3 + [
            pl.BlockSpec((1, pieces * width), lambda i: (0, i)),
            pl.BlockSpec((1, HD), lambda i: (0, 0)),
        ]
        small = (
            jax.ShapeDtypeStruct((1, slots, full_width), BF16),
            jax.ShapeDtypeStruct((1, slots), BF16),
        )
        small_specs = (
            pl.BlockSpec((1, slots, pieces * width), lambda i: (0, 0, i)),
            pl.BlockSpec((1, slots), lambda i: (0, 0)),
        )
    else:
        small = (
            jax.ShapeDtypeStruct((1, full_width), F32),
            jax.ShapeDtypeStruct((1, HD), F32),
        )
        small_specs = (
            pl.BlockSpec((1, pieces * width), lambda i: (0, i)),
            pl.BlockSpec((1, HD), lambda i: (0, 0)),
        )

    def body(weight_ref, kept_ref, main_ref, side_ref, *refs):
        refs = refs[3:] if previous else refs
        unpack_body(slot, entries, weight_ref, kept_ref, main_ref, side_ref, *refs)

    return pl.pallas_call(
        body,
        grid=(heads // pieces,),
        out_shape=(whole, whole, whole) + small,
        in_specs=in_specs,
        out_specs=(part, part, part) + small_specs,
        input_output_aliases={4 + at: at for at in range(3)} if previous else {},
        compiler_params=pltpu.CompilerParams(vmem_limit_bytes=VMEM_LIMIT),
        cost_estimate=pl.CostEstimate(
            flops=3 * tokens * full_width,
            bytes_accessed=12 * tokens * full_width,
            transcendentals=0,
        ),
    )(weight, kept, returned, returned, *previous)


def exchange(pieces):
    return lax.all_to_all(pieces, ("expert", "seq"), split_axis=0, concat_axis=0, tiled=True)


def sum_over_replicas(values):
    replicas = lax.axis_size("rep")
    total = values
    for shift in range(1, replicas):
        total = total + lax.ppermute(
            values, "rep", [(at, (at + shift) % replicas) for at in range(replicas)]
        )
    return total


def local(
    query_in,
    key_in,
    value_in,
    sample_noise,
    old_velocity,
    gate_scale,
    rewards,
    group_ids,
    timesteps,
    counts,
):
    slots = query_in.shape[1]
    tokens = query_in.shape[2]
    full_width = query_in.shape[3]
    groups = lax.axis_size("seq")
    sets = lax.axis_size("expert")
    heads = sets * groups
    width = full_width // heads
    expert_at = lax.axis_index("expert")

    def own_expert(both):
        return lax.dynamic_index_in_dim(both, expert_at, 0, keepdims=False)

    arrays = (query_in, key_in, value_in, sample_noise, old_velocity)
    kept_mask = (
        jnp.arange(slots, dtype=jnp.int32)[None, :] < counts[:, 0][:, None]
    ).astype(F32)
    choose = (group_ids[..., None] == jnp.arange(GROUPS, dtype=jnp.int32)).astype(F32)
    live_mask = choose * kept_mask[..., None]
    sums = sum_over_replicas(
        jnp.stack(
            (
                jnp.sum(live_mask, axis=(0, 1)),
                jnp.sum(live_mask * rewards[..., None], axis=(0, 1)),
                jnp.sum(live_mask * (rewards * rewards)[..., None], axis=(0, 1)),
            )
        )
    )
    number, reward_sum, square = sums[0], sums[1], sums[2]
    group_mean = reward_sum / jnp.maximum(number, 1.0)
    spread = square / jnp.maximum(number, 1.0) - group_mean * group_mean
    centre = jnp.sum(choose * group_mean, axis=-1)
    group_scale = jnp.sum(choose * jnp.sqrt(jnp.maximum(spread, 1.0)), axis=-1)
    advantage = (rewards - centre) / group_scale
    kept_here = own_expert(kept_mask)
    weight = own_expert(kept_mask * advantage)

    arrived, misfits = [], []
    for slot in range(slots):
        packed, misfit = pack(
            slot, timesteps, arrays, gate_scale if slot == 0 else None, heads
        )
        arrived.append(exchange(packed).reshape((sets, groups) + packed.shape[1:]))
        misfits.append(misfit)
    returned = []
    for slot in range(slots):
        sent = attention(
            slot, timesteps, arrived[slot], arrived[0], misfits[slot]
        )
        returned.append(exchange(sent.reshape(heads, 3 * tokens + SIDE, width)))
    held = ()
    for slot in range(slots):
        held = unpack(slot, slots, weight, kept_here, returned[slot], held)
    return held


def solution(mesh):
    placed = (
        P("expert", "rep", "seq", None),
        P("expert", "rep", "seq", None),
        P("expert", "rep", "seq", None),
        P("expert", "rep", "seq", None),
        P("expert", "rep", "seq", None),
        P("expert", "rep", None),
        P(None, "rep"),
        P(None, "rep"),
        P(None, "rep"),
        P(None, "rep"),
    )
    return jax.shard_map(
        local,
        mesh=mesh,
        in_specs=placed,
        out_specs=(
            P("expert", "rep", "seq", None),
            P("expert", "rep", "seq", None),
            P("expert", "rep", "seq", None),
            P("expert", "rep", None),
            P("expert", "rep"),
        ),
        check_vma=False,
    )
```

```python
import functools

import jax
import jax.numpy as jnp
from jax import lax
from jax.experimental import pallas as pl
from jax.experimental.pallas import tpu as pltpu
from jax.sharding import PartitionSpec as P

HD = 128
GROUPS = 4
GATE_ROWS = 16
SIDE = 16
F32 = jnp.float32
BF16 = jnp.bfloat16
NN = (((1,), (0,)), ((), ()))
NT = (((1,), (1,)), ((), ()))
VMEM_LIMIT = 63 * 1024 * 1024


def step_coef(timestep, shape):
    fraction = jnp.full(shape, timestep.astype(F32)) / 1000.0
    sigma_level = 0.7 * jnp.sqrt(fraction / (1.0 - fraction))
    return jnp.sqrt(jnp.float32(0.1)) / sigma_level


def dot(left, right, dims=NN):
    return lax.dot_general(left, right, dims, preferred_element_type=F32)


def fold_rows(values, reduce):
    rows, columns = values.shape
    return reduce(values.reshape(rows // 8, 8, columns), axis=0)


def pack_body(
    slot, steps_ref, query_ref, key_ref, value_ref, noise_ref, old_ref, *refs
):
    out_ref, misfit_ref = refs[-2:]
    pieces, _, width = out_ref.shape
    tokens = query_ref.shape[2]
    coefficient = step_coef(steps_ref[lax.axis_index("expert"), slot], (8, width))[0:1]

    @pl.when(pl.program_id(0) == 0)
    def _():
        misfit_ref[...] = jnp.zeros_like(misfit_ref)

    total = misfit_ref[...]
    for piece in range(pieces):
        columns = slice(piece * width, (piece + 1) * width)
        out_ref[piece, 0:tokens] = query_ref[0, 0, :, columns]
        out_ref[piece, tokens : 2 * tokens] = key_ref[0, 0, :, columns]
        out_ref[piece, 2 * tokens : 3 * tokens] = value_ref[0, 0, :, columns]
        noise = noise_ref[0, 0, :, columns].astype(F32)
        shift = coefficient * old_ref[0, 0, :, columns].astype(F32)
        out_ref[piece, 3 * tokens : 4 * tokens] = (noise - shift).astype(BF16)
        total = total + fold_rows(shift * (shift - 2.0 * noise), jnp.sum)
        for gate_ref in refs[:-2]:
            gates = gate_ref[0, :, columns]
            blank = jnp.zeros((GATE_ROWS - gates.shape[0], width), BF16)
            out_ref[piece, 4 * tokens :] = jnp.concatenate([gates, blank], axis=0)
    misfit_ref[...] = total


def pack(slot, timesteps, arrays, gate_scale, groups):
    _, _, tokens, full_width = arrays[0].shape
    width = full_width // groups
    pieces = 16
    rows = pl.BlockSpec((1, 1, tokens, pieces * width), lambda i: (0, slot, 0, i))
    gates = [] if gate_scale is None else [gate_scale]
    held = 4 * tokens + GATE_ROWS * len(gates)
    return pl.pallas_call(
        functools.partial(pack_body, slot),
        grid=(groups // pieces,),
        out_shape=(
            jax.ShapeDtypeStruct((groups, held, width), BF16),
            jax.ShapeDtypeStruct((8, width), F32),
        ),
        in_specs=[pl.BlockSpec(memory_space=pltpu.SMEM)]
        + [rows] * 5
        + [pl.BlockSpec((1,) + g.shape[1:2] + (pieces * width,), lambda i: (0, 0, i)) for g in gates],
        out_specs=(
            pl.BlockSpec((pieces, held, width), lambda i: (i, 0, 0)),
            pl.BlockSpec((8, width), lambda i: (0, 0)),
        ),
        compiler_params=pltpu.CompilerParams(vmem_limit_bytes=VMEM_LIMIT),
        cost_estimate=pl.CostEstimate(
            flops=6 * tokens * full_width,
            bytes_accessed=18 * tokens * full_width,
            transcendentals=0,
        ),
    )(timesteps, *arrays, *gates)


def attention_body(
    slot,
    block_rows,
    chunk,
    steps_ref,
    query_ref,
    key_ref,
    value_ref,
    field_ref,
    gate_ref,
    misfit_ref,
    out_ref,
    q_rows,
    k_rows,
    v_rows,
    k_cols,
    v_cols,
    field_cols,
    scores,
    weights,
    key_total,
    value_total,
    gate_total,
    misfit_total,
):
    length = q_rows.shape[0]
    pieces = out_ref.shape[1]
    tokens = length // pieces
    step_set = pl.program_id(0)
    scale_factor = HD ** (-0.5)
    log2e = 1.4426950408889634
    coefficient = step_coef(steps_ref[step_set, slot], (8, block_rows))[0:1]
    q_rows[...] = query_ref[...].reshape(length, HD)
    k_rows[...] = key_ref[...].reshape(length, HD)
    v_rows[...] = value_ref[...].reshape(length, HD)
    k_cols[...] = k_rows[...].T
    v_cols[...] = v_rows[...].T
    field_cols[...] = field_ref[...].reshape(length, HD).T
    gate_row = gate_ref[0, 0, slot : slot + 1, :].astype(F32)
    gate = jnp.broadcast_to(gate_row, (8, HD)).T[:, 0:1]
    gate_total[...] = jnp.zeros_like(gate_total)
    misfit_total[...] = jnp.zeros_like(misfit_total)
    chunks = [slice(at, at + chunk) for at in range(0, length, chunk)]

    def one_block(index, _):
        first = index == 0
        start = pl.multiple_of(index * block_rows, block_rows)
        rows_query = q_rows[pl.ds(start, block_rows), :]
        top = jnp.full((8, block_rows), -jnp.inf, F32)
        for part in chunks:
            block_scores = dot(k_rows[part, :], rows_query, NT)
            scores[part, :] = block_scores
            top = jnp.maximum(top, fold_rows(block_scores, jnp.max))
        row_max = jnp.max(top, axis=0, keepdims=True)
        sums = jnp.zeros((8, block_rows), F32)
        for part in chunks:
            raised = jnp.exp2((scores[part, :] - row_max) * (scale_factor * log2e))
            sums = sums + fold_rows(raised, jnp.sum)
            scores[part, :] = raised
        inverse = 1.0 / jnp.sum(sums, axis=0, keepdims=True)
        mixed = jnp.zeros((HD, block_rows), F32)
        for part in chunks:
            rounded = (scores[part, :] * inverse).astype(BF16)
            weights[part, :] = rounded
            mixed = mixed + dot(v_cols[:, part], rounded)
        attended = mixed.astype(BF16).astype(F32)
        field = field_cols[:, pl.ds(start, block_rows)].astype(F32)
        moved = coefficient * (gate * attended)
        misfit_total[...] += moved * (2.0 * field + moved)
        grad_gap = coefficient * (field + moved)
        gate_total[...] += grad_gap * attended
        grad_cols = (grad_gap * gate).astype(BF16)
        grad_rows = grad_cols.T
        row_dot = jnp.sum(grad_cols.astype(F32) * attended, axis=0, keepdims=True)
        grad_query = jnp.zeros((HD, block_rows), F32)
        for part in chunks:
            rounded = weights[part, :]
            grad_probs = dot(v_rows[part, :], grad_cols)
            grad_scores = (rounded.astype(F32) * (grad_probs - row_dot)).astype(BF16)
            grad_query = grad_query + dot(k_cols[:, part], grad_scores)
            value_part = dot(rounded, grad_rows)
            key_part = dot(grad_scores, rows_query)
            value_total[part, :] = jnp.where(first, value_part, value_total[part, :] + value_part)
            key_total[part, :] = jnp.where(first, key_part, key_total[part, :] + key_part)
        held = block_rows // tokens
        out_ref[0, pl.ds(index * held, held), 0:tokens, :] = (
            (grad_query.T * scale_factor).astype(BF16).reshape(held, tokens, HD)
        )
        return 0

    lax.fori_loop(0, length // block_rows, one_block, 0)
    out_ref[0, :, tokens : 2 * tokens, :] = (
        (key_total[...] * scale_factor).astype(BF16).reshape(pieces, tokens, HD)
    )
    out_ref[0, :, 2 * tokens : 3 * tokens, :] = (
        value_total[...].astype(BF16).reshape(pieces, tokens, HD)
    )

    def row_of(values):
        total = values[:, 0:HD]
        for at in range(HD, values.shape[1], HD):
            total = total + values[:, at : at + HD]
        return jnp.sum(total.T, axis=0, keepdims=True)

    gate_row = row_of(gate_total[...])
    local_row = jnp.sum(misfit_ref[...], axis=0, keepdims=True)
    misfit_row = row_of(misfit_total[...]) + jnp.where(step_set == lax.axis_index("expert"), local_row, 0.0)
    rest = misfit_row
    side = []
    for _ in range(3):
        side.append(rest.astype(BF16).astype(F32))
        rest = rest - side[-1]
    gate_high = gate_row.astype(BF16).astype(F32)
    row_at = lax.broadcasted_iota(jnp.int32, (SIDE, HD), 0)
    rows = jnp.zeros((SIDE, HD), F32)
    for at, row in enumerate([gate_high, gate_row - gate_high] + side):
        rows = jnp.where(row_at == at, row, rows)
    out_ref[0, :, 3 * tokens :, :] = jnp.broadcast_to(
        rows.astype(BF16)[None], (pieces, SIDE, HD)
    )


def attention(slot, timesteps, arrived, gates, misfit):
    sets, groups, _, width = arrived.shape
    tokens = arrived.shape[2] // (4 * GATE_ROWS) * GATE_ROWS
    length = groups * tokens
    block_rows, chunk = 512, 512

    def field(which):
        return pl.BlockSpec((1, groups, tokens, HD), lambda e: (e, 0, which, 0))

    return pl.pallas_call(
        functools.partial(attention_body, slot, block_rows, chunk),
        grid=(sets,),
        out_shape=jax.ShapeDtypeStruct((sets, groups, 3 * tokens + SIDE, width), BF16),
        in_specs=[pl.BlockSpec(memory_space=pltpu.SMEM)]
        + [field(which) for which in range(4)]
        + [
            pl.BlockSpec((1, 1, GATE_ROWS, HD), lambda e: (e, 0, 4 * tokens // GATE_ROWS, 0)),
            pl.BlockSpec((8, HD), lambda e: (0, 0)),
        ],
        out_specs=pl.BlockSpec((1, groups, 3 * tokens + SIDE, HD), lambda e: (e, 0, 0, 0)),
        scratch_shapes=[pltpu.VMEM((length, HD), BF16)] * 3
        + [pltpu.VMEM((HD, length), BF16)] * 3
        + [
            pltpu.VMEM((length, block_rows), F32),
            pltpu.VMEM((length, block_rows), BF16),
            pltpu.VMEM((length, HD), F32),
            pltpu.VMEM((length, HD), F32),
            pltpu.VMEM((HD, block_rows), F32),
            pltpu.VMEM((HD, block_rows), F32),
        ],
        compiler_params=pltpu.CompilerParams(vmem_limit_bytes=VMEM_LIMIT),
        cost_estimate=pl.CostEstimate(
            flops=sets * 24 * length * length * HD,
            bytes_accessed=sets * 14 * length * width,
            transcendentals=sets * length * length,
        ),
    )(timesteps, arrived, arrived, arrived, arrived, gates, misfit)


def unpack_body(slot, entries, weight_ref, kept_ref, main_ref, side_ref, *refs):
    query_ref, key_ref, value_ref, gate_ref, log_ref = refs[-5:]
    earlier = refs[:-5]
    pieces = main_ref.shape[0]
    width = main_ref.shape[2]
    tokens = query_ref.shape[2]
    misfit = jnp.sum(side_ref[:, 2:5, :].astype(F32))
    ratio_log = jnp.full((1, HD), -misfit / (2.0 * entries), F32)
    if earlier:
        gate_ref[0, 0:1, :] = earlier[0][...].astype(BF16)
        own_log = ratio_log[:, 0:1] * kept_ref[slot]
        log_ref[...] = jnp.concatenate([earlier[1][:, 0:1], own_log], axis=1).astype(BF16)
    else:
        log_ref[...] = ratio_log * kept_ref[slot]
    factor = weight_ref[slot] * jnp.exp(ratio_log)
    first = pl.program_id(0) * pieces
    for piece in range(pieces):
        columns = slice(piece * width, (piece + 1) * width)
        parts = side_ref[first + piece, 0:2, :].astype(F32)
        gate_row = (parts[0:1] + parts[1:2]) * factor
        if earlier:
            gate_ref[0, 1:2, columns] = gate_row.astype(BF16)
        else:
            gate_ref[:, columns] = gate_row
        for which, out_ref in enumerate((query_ref, key_ref, value_ref)):
            rows = main_ref[piece, which * tokens : (which + 1) * tokens, :].astype(F32)
            out_ref[0, 0, :, columns] = (rows * factor).astype(BF16)


def unpack(slot, slots, weight, kept, returned, previous):
    heads, rows, width = returned.shape
    tokens = (rows - SIDE) // 3
    full_width = heads * width
    entries = full_width * tokens * lax.axis_size("seq")
    pieces = 16
    whole = jax.ShapeDtypeStruct((1, slots, tokens, full_width), BF16)
    part = pl.BlockSpec((1, 1, tokens, pieces * width), lambda i: (0, slot, 0, i))
    in_specs = [
        pl.BlockSpec(memory_space=pltpu.SMEM),
        pl.BlockSpec(memory_space=pltpu.SMEM),
        pl.BlockSpec((pieces, 3 * tokens, width), lambda i: (i, 0, 0)),
        pl.BlockSpec((heads, SIDE, width), lambda i: (0, 3 * tokens // SIDE, 0)),
    ]
    if previous:
        in_specs += [pl.BlockSpec(memory_space=pl.ANY)] * 3 + [
            pl.BlockSpec((1, pieces * width), lambda i: (0, i)),
            pl.BlockSpec((1, HD), lambda i: (0, 0)),
        ]
        small = (
            jax.ShapeDtypeStruct((1, slots, full_width), BF16),
            jax.ShapeDtypeStruct((1, slots), BF16),
        )
        small_specs = (
            pl.BlockSpec((1, slots, pieces * width), lambda i: (0, 0, i)),
            pl.BlockSpec((1, slots), lambda i: (0, 0)),
        )
    else:
        small = (
            jax.ShapeDtypeStruct((1, full_width), F32),
            jax.ShapeDtypeStruct((1, HD), F32),
        )
        small_specs = (
            pl.BlockSpec((1, pieces * width), lambda i: (0, i)),
            pl.BlockSpec((1, HD), lambda i: (0, 0)),
        )

    def body(weight_ref, kept_ref, main_ref, side_ref, *refs):
        refs = refs[3:] if previous else refs
        unpack_body(slot, entries, weight_ref, kept_ref, main_ref, side_ref, *refs)

    return pl.pallas_call(
        body,
        grid=(heads // pieces,),
        out_shape=(whole, whole, whole) + small,
        in_specs=in_specs,
        out_specs=(part, part, part) + small_specs,
        input_output_aliases={4 + at: at for at in range(3)} if previous else {},
        compiler_params=pltpu.CompilerParams(vmem_limit_bytes=VMEM_LIMIT),
        cost_estimate=pl.CostEstimate(
            flops=3 * tokens * full_width,
            bytes_accessed=12 * tokens * full_width,
            transcendentals=0,
        ),
    )(weight, kept, returned, returned, *previous)


def exchange(pieces):
    return lax.all_to_all(pieces, ("expert", "seq"), split_axis=0, concat_axis=0, tiled=True)


def sum_over_replicas(values):
    replicas = lax.axis_size("rep")
    total = values
    for shift in range(1, replicas):
        total = total + lax.ppermute(
            values, "rep", [(at, (at + shift) % replicas) for at in range(replicas)]
        )
    return total


def local(
    query_in,
    key_in,
    value_in,
    sample_noise,
    old_velocity,
    gate_scale,
    rewards,
    group_ids,
    timesteps,
    counts,
):
    slots = query_in.shape[1]
    tokens = query_in.shape[2]
    full_width = query_in.shape[3]
    groups = lax.axis_size("seq")
    sets = lax.axis_size("expert")
    heads = sets * groups
    width = full_width // heads
    expert_at = lax.axis_index("expert")

    def own_expert(both):
        return lax.dynamic_index_in_dim(both, expert_at, 0, keepdims=False)

    arrays = (query_in, key_in, value_in, sample_noise, old_velocity)
    kept_mask = (
        jnp.arange(slots, dtype=jnp.int32)[None, :] < counts[:, 0][:, None]
    ).astype(F32)
    choose = (group_ids[..., None] == jnp.arange(GROUPS, dtype=jnp.int32)).astype(F32)
    live_mask = choose * kept_mask[..., None]
    sums = sum_over_replicas(
        jnp.stack(
            (
                jnp.sum(live_mask, axis=(0, 1)),
                jnp.sum(live_mask * rewards[..., None], axis=(0, 1)),
                jnp.sum(live_mask * (rewards * rewards)[..., None], axis=(0, 1)),
            )
        )
    )
    number, reward_sum, square = sums[0], sums[1], sums[2]
    group_mean = reward_sum / jnp.maximum(number, 1.0)
    spread = square / jnp.maximum(number, 1.0) - group_mean * group_mean
    centre = jnp.sum(choose * group_mean, axis=-1)
    group_scale = jnp.sum(choose * jnp.sqrt(jnp.maximum(spread, 1.0)), axis=-1)
    advantage = (rewards - centre) / group_scale
    kept_here = own_expert(kept_mask)
    weight = own_expert(kept_mask * advantage)

    arrived, misfits = [], []
    for slot in range(slots):
        packed, misfit = pack(
            slot, timesteps, arrays, gate_scale if slot == 0 else None, heads
        )
        arrived.append(exchange(packed).reshape((sets, groups) + packed.shape[1:]))
        misfits.append(misfit)
    returned = []
    for slot in range(slots):
        sent = attention(
            slot, timesteps, arrived[slot], arrived[0], misfits[slot]
        )
        returned.append(exchange(sent.reshape(heads, 3 * tokens + SIDE, width)))
    held = ()
    for slot in range(slots):
        held = unpack(slot, slots, weight, kept_here, returned[slot], held)
    return held


def solution(mesh):
    placed = (
        P("expert", "rep", "seq", None),
        P("expert", "rep", "seq", None),
        P("expert", "rep", "seq", None),
        P("expert", "rep", "seq", None),
        P("expert", "rep", "seq", None),
        P("expert", "rep", None),
        P(None, "rep"),
        P(None, "rep"),
        P(None, "rep"),
        P(None, "rep"),
    )
    return jax.shard_map(
        local,
        mesh=mesh,
        in_specs=placed,
        out_specs=(
            P("expert", "rep", "seq", None),
            P("expert", "rep", "seq", None),
            P("expert", "rep", "seq", None),
            P("expert", "rep", None),
            P("expert", "rep"),
        ),
        check_vma=False,
    )
```

```python
import functools

import jax
import jax.numpy as jnp
from jax import lax
from jax.experimental import pallas as pl
from jax.experimental.pallas import tpu as pltpu
from jax.sharding import PartitionSpec as P

HD = 128
GROUPS = 4
SIDE = 16
F32 = jnp.float32
BF16 = jnp.bfloat16
NN = (((1,), (0,)), ((), ()))
NT = (((1,), (1,)), ((), ()))
VMEM_LIMIT = 63 * 1024 * 1024


def step_coef(timestep, shape):
    fraction = jnp.full(shape, timestep.astype(F32)) / 1000.0
    sigma_level = 0.7 * jnp.sqrt(fraction / (1.0 - fraction))
    return jnp.sqrt(jnp.float32(0.1)) / sigma_level


def dot(left, right, dims=NN):
    return lax.dot_general(left, right, dims, preferred_element_type=F32)


def fold_rows(values, reduce):
    rows, columns = values.shape
    return reduce(values.reshape(rows // 8, 8, columns), axis=0)


def pack_body(
    slot, steps_ref, query_ref, key_ref, value_ref, noise_ref, old_ref, out_ref, misfit_ref
):
    pieces, _, width = out_ref.shape
    tokens = query_ref.shape[2]
    coefficient = step_coef(steps_ref[lax.axis_index("expert"), slot], (8, width))[0:1]

    @pl.when(pl.program_id(0) == 0)
    def _():
        misfit_ref[...] = jnp.zeros_like(misfit_ref)

    total = misfit_ref[...]
    for piece in range(pieces):
        columns = slice(piece * width, (piece + 1) * width)
        out_ref[piece, 0:tokens] = query_ref[0, 0, :, columns]
        out_ref[piece, tokens : 2 * tokens] = key_ref[0, 0, :, columns]
        out_ref[piece, 2 * tokens : 3 * tokens] = value_ref[0, 0, :, columns]
        noise = noise_ref[0, 0, :, columns].astype(F32)
        shift = coefficient * old_ref[0, 0, :, columns].astype(F32)
        out_ref[piece, 3 * tokens : 4 * tokens] = (noise - shift).astype(BF16)
        total = total + fold_rows(shift * (shift - 2.0 * noise), jnp.sum)
    misfit_ref[...] = total


def pack(slot, timesteps, arrays, groups):
    _, _, tokens, full_width = arrays[0].shape
    width = full_width // groups
    pieces = 16
    rows = pl.BlockSpec((1, 1, tokens, pieces * width), lambda i: (0, slot, 0, i))
    held = 4 * tokens
    return pl.pallas_call(
        functools.partial(pack_body, slot),
        grid=(groups // pieces,),
        out_shape=(
            jax.ShapeDtypeStruct((groups, held, width), BF16),
            jax.ShapeDtypeStruct((8, width), F32),
        ),
        in_specs=[pl.BlockSpec(memory_space=pltpu.SMEM)] + [rows] * 5,
        out_specs=(
            pl.BlockSpec((pieces, held, width), lambda i: (i, 0, 0)),
            pl.BlockSpec((8, width), lambda i: (0, 0)),
        ),
        compiler_params=pltpu.CompilerParams(vmem_limit_bytes=VMEM_LIMIT),
        cost_estimate=pl.CostEstimate(
            flops=6 * tokens * full_width,
            bytes_accessed=18 * tokens * full_width,
            transcendentals=0,
        ),
    )(timesteps, *arrays)


def attention_body(
    slot,
    block_rows,
    chunk,
    steps_ref,
    query_ref,
    key_ref,
    value_ref,
    field_ref,
    gate_ref,
    misfit_ref,
    out_ref,
    q_rows,
    k_rows,
    v_rows,
    k_cols,
    v_cols,
    field_cols,
    scores,
    weights,
    key_total,
    value_total,
    gate_total,
    misfit_total,
):
    length = q_rows.shape[0]
    pieces = out_ref.shape[1]
    tokens = length // pieces
    step_set = pl.program_id(0)
    scale_factor = HD ** (-0.5)
    log2e = 1.4426950408889634
    coefficient = step_coef(steps_ref[step_set, slot], (8, block_rows))[0:1]
    q_rows[...] = query_ref[...].reshape(length, HD)
    k_rows[...] = key_ref[...].reshape(length, HD)
    v_rows[...] = value_ref[...].reshape(length, HD)
    k_cols[...] = k_rows[...].T
    v_cols[...] = v_rows[...].T
    field_cols[...] = field_ref[...].reshape(length, HD).T
    gate_row = gate_ref[0, slot : slot + 1, :].astype(F32)
    gate = jnp.broadcast_to(gate_row, (8, HD)).T[:, 0:1]
    gate_total[...] = jnp.zeros_like(gate_total)
    misfit_total[...] = jnp.zeros_like(misfit_total)
    chunks = [slice(at, at + chunk) for at in range(0, length, chunk)]

    def one_block(index, _):
        first = index == 0
        start = pl.multiple_of(index * block_rows, block_rows)
        rows_query = q_rows[pl.ds(start, block_rows), :]
        top = jnp.full((8, block_rows), -jnp.inf, F32)
        for part in chunks:
            block_scores = dot(k_rows[part, :], rows_query, NT)
            scores[part, :] = block_scores
            top = jnp.maximum(top, fold_rows(block_scores, jnp.max))
        row_max = jnp.max(top, axis=0, keepdims=True)
        sums = jnp.zeros((8, block_rows), F32)
        for part in chunks:
            raised = jnp.exp2((scores[part, :] - row_max) * (scale_factor * log2e))
            sums = sums + fold_rows(raised, jnp.sum)
            scores[part, :] = raised
        inverse = 1.0 / jnp.sum(sums, axis=0, keepdims=True)
        mixed = jnp.zeros((HD, block_rows), F32)
        for part in chunks:
            rounded = (scores[part, :] * inverse).astype(BF16)
            weights[part, :] = rounded
            mixed = mixed + dot(v_cols[:, part], rounded)
        attended = mixed.astype(BF16).astype(F32)
        field = field_cols[:, pl.ds(start, block_rows)].astype(F32)
        moved = coefficient * (gate * attended)
        misfit_total[...] += moved * (2.0 * field + moved)
        grad_gap = coefficient * (field + moved)
        gate_total[...] += grad_gap * attended
        grad_cols = (grad_gap * gate).astype(BF16)
        grad_rows = grad_cols.T
        row_dot = jnp.sum(grad_cols.astype(F32) * attended, axis=0, keepdims=True)
        grad_query = jnp.zeros((HD, block_rows), F32)
        for part in chunks:
            rounded = weights[part, :]
            grad_probs = dot(v_rows[part, :], grad_cols)
            grad_scores = (rounded.astype(F32) * (grad_probs - row_dot)).astype(BF16)
            grad_query = grad_query + dot(k_cols[:, part], grad_scores)
            value_part = dot(rounded, grad_rows)
            key_part = dot(grad_scores, rows_query)
            value_total[part, :] = jnp.where(first, value_part, value_total[part, :] + value_part)
            key_total[part, :] = jnp.where(first, key_part, key_total[part, :] + key_part)
        held = block_rows // tokens
        out_ref[0, pl.ds(index * held, held), 0:tokens, :] = (
            (grad_query.T * scale_factor).astype(BF16).reshape(held, tokens, HD)
        )
        return 0

    lax.fori_loop(0, length // block_rows, one_block, 0)
    out_ref[0, :, tokens : 2 * tokens, :] = (
        (key_total[...] * scale_factor).astype(BF16).reshape(pieces, tokens, HD)
    )
    out_ref[0, :, 2 * tokens : 3 * tokens, :] = (
        value_total[...].astype(BF16).reshape(pieces, tokens, HD)
    )

    def row_of(values):
        total = values[:, 0:HD]
        for at in range(HD, values.shape[1], HD):
            total = total + values[:, at : at + HD]
        return jnp.sum(total.T, axis=0, keepdims=True)

    gate_row = row_of(gate_total[...])
    local_row = jnp.sum(misfit_ref[...], axis=0, keepdims=True)
    misfit_row = row_of(misfit_total[...]) + jnp.where(step_set == lax.axis_index("expert"), local_row, 0.0)
    rest = misfit_row
    side = []
    for _ in range(3):
        side.append(rest.astype(BF16).astype(F32))
        rest = rest - side[-1]
    gate_high = gate_row.astype(BF16).astype(F32)
    row_at = lax.broadcasted_iota(jnp.int32, (SIDE, HD), 0)
    rows = jnp.zeros((SIDE, HD), F32)
    for at, row in enumerate([gate_high, gate_row - gate_high] + side):
        rows = jnp.where(row_at == at, row, rows)
    out_ref[0, :, 3 * tokens :, :] = jnp.broadcast_to(
        rows.astype(BF16)[None], (pieces, SIDE, HD)
    )


def attention(slot, timesteps, arrived, gates, misfit):
    sets, groups, _, width = arrived.shape
    tokens = arrived.shape[2] // 4
    length = groups * tokens
    block_rows, chunk = 512, 512

    def field(which):
        return pl.BlockSpec((1, groups, tokens, HD), lambda e: (e, 0, which, 0))

    return pl.pallas_call(
        functools.partial(attention_body, slot, block_rows, chunk),
        grid=(sets,),
        out_shape=jax.ShapeDtypeStruct((sets, groups, 3 * tokens + SIDE, width), BF16),
        in_specs=[pl.BlockSpec(memory_space=pltpu.SMEM)]
        + [field(which) for which in range(4)]
        + [
            pl.BlockSpec((1,) + gates.shape[1:], lambda e: (e, 0, 0)),
            pl.BlockSpec((8, HD), lambda e: (0, 0)),
        ],
        out_specs=pl.BlockSpec((1, groups, 3 * tokens + SIDE, HD), lambda e: (e, 0, 0, 0)),
        scratch_shapes=[pltpu.VMEM((length, HD), BF16)] * 3
        + [pltpu.VMEM((HD, length), BF16)] * 3
        + [
            pltpu.VMEM((length, block_rows), F32),
            pltpu.VMEM((length, block_rows), BF16),
            pltpu.VMEM((length, HD), F32),
            pltpu.VMEM((length, HD), F32),
            pltpu.VMEM((HD, block_rows), F32),
            pltpu.VMEM((HD, block_rows), F32),
        ],
        compiler_params=pltpu.CompilerParams(vmem_limit_bytes=VMEM_LIMIT),
        cost_estimate=pl.CostEstimate(
            flops=sets * 24 * length * length * HD,
            bytes_accessed=sets * 14 * length * width,
            transcendentals=sets * length * length,
        ),
    )(timesteps, arrived, arrived, arrived, arrived, gates, misfit)


def unpack_body(slot, entries, weight_ref, kept_ref, main_ref, side_ref, *refs):
    query_ref, key_ref, value_ref, gate_ref, log_ref = refs[-5:]
    earlier = refs[:-5]
    pieces = main_ref.shape[0]
    width = main_ref.shape[2]
    tokens = query_ref.shape[2]
    misfit = jnp.sum(side_ref[:, 2:5, :].astype(F32))
    ratio_log = jnp.full((1, HD), -misfit / (2.0 * entries), F32)
    if earlier:
        gate_ref[0, 0:1, :] = earlier[0][...].astype(BF16)
        own_log = ratio_log[:, 0:1] * kept_ref[slot]
        log_ref[...] = jnp.concatenate([earlier[1][:, 0:1], own_log], axis=1).astype(BF16)
    else:
        log_ref[...] = ratio_log * kept_ref[slot]
    factor = weight_ref[slot] * jnp.exp(ratio_log)
    first = pl.program_id(0) * pieces
    for piece in range(pieces):
        columns = slice(piece * width, (piece + 1) * width)
        parts = side_ref[first + piece, 0:2, :].astype(F32)
        gate_row = (parts[0:1] + parts[1:2]) * factor
        if earlier:
            gate_ref[0, 1:2, columns] = gate_row.astype(BF16)
        else:
            gate_ref[:, columns] = gate_row
        for which, out_ref in enumerate((query_ref, key_ref, value_ref)):
            rows = main_ref[piece, which * tokens : (which + 1) * tokens, :].astype(F32)
            out_ref[0, 0, :, columns] = (rows * factor).astype(BF16)


def unpack(slot, slots, weight, kept, returned, previous):
    heads, rows, width = returned.shape
    tokens = (rows - SIDE) // 3
    full_width = heads * width
    entries = full_width * tokens * lax.axis_size("seq")
    pieces = 16
    whole = jax.ShapeDtypeStruct((1, slots, tokens, full_width), BF16)
    part = pl.BlockSpec((1, 1, tokens, pieces * width), lambda i: (0, slot, 0, i))
    in_specs = [
        pl.BlockSpec(memory_space=pltpu.SMEM),
        pl.BlockSpec(memory_space=pltpu.SMEM),
        pl.BlockSpec((pieces, 3 * tokens, width), lambda i: (i, 0, 0)),
        pl.BlockSpec((heads, SIDE, width), lambda i: (0, 3 * tokens // SIDE, 0)),
    ]
    if previous:
        in_specs += [pl.BlockSpec(memory_space=pl.ANY)] * 3 + [
            pl.BlockSpec((1, pieces * width), lambda i: (0, i)),
            pl.BlockSpec((1, HD), lambda i: (0, 0)),
        ]
        small = (
            jax.ShapeDtypeStruct((1, slots, full_width), BF16),
            jax.ShapeDtypeStruct((1, slots), BF16),
        )
        small_specs = (
            pl.BlockSpec((1, slots, pieces * width), lambda i: (0, 0, i)),
            pl.BlockSpec((1, slots), lambda i: (0, 0)),
        )
    else:
        small = (
            jax.ShapeDtypeStruct((1, full_width), F32),
            jax.ShapeDtypeStruct((1, HD), F32),
        )
        small_specs = (
            pl.BlockSpec((1, pieces * width), lambda i: (0, i)),
            pl.BlockSpec((1, HD), lambda i: (0, 0)),
        )

    def body(weight_ref, kept_ref, main_ref, side_ref, *refs):
        refs = refs[3:] if previous else refs
        unpack_body(slot, entries, weight_ref, kept_ref, main_ref, side_ref, *refs)

    return pl.pallas_call(
        body,
        grid=(heads // pieces,),
        out_shape=(whole, whole, whole) + small,
        in_specs=in_specs,
        out_specs=(part, part, part) + small_specs,
        input_output_aliases={4 + at: at for at in range(3)} if previous else {},
        compiler_params=pltpu.CompilerParams(vmem_limit_bytes=VMEM_LIMIT),
        cost_estimate=pl.CostEstimate(
            flops=3 * tokens * full_width,
            bytes_accessed=12 * tokens * full_width,
            transcendentals=0,
        ),
    )(weight, kept, returned, returned, *previous)


def exchange(pieces):
    return lax.all_to_all(pieces, ("expert", "seq"), split_axis=0, concat_axis=0, tiled=True)


def sum_over_replicas(values):
    replicas = lax.axis_size("rep")
    total = values
    for shift in range(1, replicas):
        total = total + lax.ppermute(
            values, "rep", [(at, (at + shift) % replicas) for at in range(replicas)]
        )
    return total


def local(
    query_in,
    key_in,
    value_in,
    sample_noise,
    old_velocity,
    gate_scale,
    rewards,
    group_ids,
    timesteps,
    counts,
):
    slots = query_in.shape[1]
    tokens = query_in.shape[2]
    full_width = query_in.shape[3]
    groups = lax.axis_size("seq")
    sets = lax.axis_size("expert")
    heads = sets * groups
    width = full_width // heads
    expert_at = lax.axis_index("expert")

    def own_expert(both):
        return lax.dynamic_index_in_dim(both, expert_at, 0, keepdims=False)

    arrays = (query_in, key_in, value_in, sample_noise, old_velocity)
    kept_mask = (
        jnp.arange(slots, dtype=jnp.int32)[None, :] < counts[:, 0][:, None]
    ).astype(F32)
    choose = (group_ids[..., None] == jnp.arange(GROUPS, dtype=jnp.int32)).astype(F32)
    live_mask = choose * kept_mask[..., None]
    sums = sum_over_replicas(
        jnp.stack(
            (
                jnp.sum(live_mask, axis=(0, 1)),
                jnp.sum(live_mask * rewards[..., None], axis=(0, 1)),
                jnp.sum(live_mask * (rewards * rewards)[..., None], axis=(0, 1)),
            )
        )
    )
    number, reward_sum, square = sums[0], sums[1], sums[2]
    group_mean = reward_sum / jnp.maximum(number, 1.0)
    spread = square / jnp.maximum(number, 1.0) - group_mean * group_mean
    centre = jnp.sum(choose * group_mean, axis=-1)
    group_scale = jnp.sum(choose * jnp.sqrt(jnp.maximum(spread, 1.0)), axis=-1)
    advantage = (rewards - centre) / group_scale
    kept_here = own_expert(kept_mask)
    weight = own_expert(kept_mask * advantage)

    gate_own = gate_scale[0]
    gate_other = lax.ppermute(gate_own, "expert", [(0, 1), (1, 0)])
    arrived, misfits = [], []
    for slot in range(slots):
        packed, misfit = pack(slot, timesteps, arrays, heads)
        if slot == 1:
            packed, gate_other = lax.optimization_barrier((packed, gate_other))
        arrived.append(exchange(packed).reshape((sets, groups) + packed.shape[1:]))
        misfits.append(misfit)
    gates = jnp.where(
        expert_at == 0, jnp.stack([gate_own, gate_other]), jnp.stack([gate_other, gate_own])
    )
    head_at = expert_at * groups + lax.axis_index("seq")
    gates = lax.dynamic_slice_in_dim(gates, head_at * width, width, 2)
    returned = []
    for slot in range(slots):
        sent = attention(
            slot, timesteps, arrived[slot], gates, misfits[slot]
        )
        returned.append(exchange(sent.reshape(heads, 3 * tokens + SIDE, width)))
    held = ()
    for slot in range(slots):
        held = unpack(slot, slots, weight, kept_here, returned[slot], held)
    return held


def solution(mesh):
    placed = (
        P("expert", "rep", "seq", None),
        P("expert", "rep", "seq", None),
        P("expert", "rep", "seq", None),
        P("expert", "rep", "seq", None),
        P("expert", "rep", "seq", None),
        P("expert", "rep", None),
        P(None, "rep"),
        P(None, "rep"),
        P(None, "rep"),
        P(None, "rep"),
    )
    return jax.shard_map(
        local,
        mesh=mesh,
        in_specs=placed,
        out_specs=(
            P("expert", "rep", "seq", None),
            P("expert", "rep", "seq", None),
            P("expert", "rep", "seq", None),
            P("expert", "rep", None),
            P("expert", "rep"),
        ),
        check_vma=False,
    )
```

```python
import functools

import jax
import jax.numpy as jnp
from jax import lax
from jax.experimental import pallas as pl
from jax.experimental.pallas import tpu as pltpu
from jax.sharding import PartitionSpec as P

HD = 128
GROUPS = 4
SIDE = 16
F32 = jnp.float32
BF16 = jnp.bfloat16
NN = (((1,), (0,)), ((), ()))
NT = (((1,), (1,)), ((), ()))
VMEM_LIMIT = 63 * 1024 * 1024
UNPACK_LIMIT = 24 * 1024 * 1024


def step_coef(timestep, shape):
    fraction = jnp.full(shape, timestep.astype(F32)) / 1000.0
    sigma_level = 0.7 * jnp.sqrt(fraction / (1.0 - fraction))
    return jnp.sqrt(jnp.float32(0.1)) / sigma_level


def dot(left, right, dims=NN):
    return lax.dot_general(left, right, dims, preferred_element_type=F32)


def fold_rows(values, reduce):
    rows, columns = values.shape
    return reduce(values.reshape(rows // 8, 8, columns), axis=0)


def pack_body(
    slot, steps_ref, query_ref, key_ref, value_ref, noise_ref, old_ref, out_ref, misfit_ref
):
    pieces, _, width = out_ref.shape
    tokens = query_ref.shape[2]
    coefficient = step_coef(steps_ref[lax.axis_index("expert"), slot], (8, width))[0:1]

    @pl.when(pl.program_id(0) == 0)
    def _():
        misfit_ref[...] = jnp.zeros_like(misfit_ref)

    total = misfit_ref[...]
    for piece in range(pieces):
        columns = slice(piece * width, (piece + 1) * width)
        out_ref[piece, 0:tokens] = query_ref[0, 0, :, columns]
        out_ref[piece, tokens : 2 * tokens] = key_ref[0, 0, :, columns]
        out_ref[piece, 2 * tokens : 3 * tokens] = value_ref[0, 0, :, columns]
        noise = noise_ref[0, 0, :, columns].astype(F32)
        shift = coefficient * old_ref[0, 0, :, columns].astype(F32)
        out_ref[piece, 3 * tokens : 4 * tokens] = (noise - shift).astype(BF16)
        total = total + fold_rows(shift * (shift - 2.0 * noise), jnp.sum)
    misfit_ref[...] = total


def pack(slot, timesteps, arrays, groups):
    _, _, tokens, full_width = arrays[0].shape
    width = full_width // groups
    pieces = 16
    rows = pl.BlockSpec((1, 1, tokens, pieces * width), lambda i: (0, slot, 0, i))
    held = 4 * tokens
    return pl.pallas_call(
        functools.partial(pack_body, slot),
        grid=(groups // pieces,),
        out_shape=(
            jax.ShapeDtypeStruct((groups, held, width), BF16),
            jax.ShapeDtypeStruct((8, width), F32),
        ),
        in_specs=[pl.BlockSpec(memory_space=pltpu.SMEM)] + [rows] * 5,
        out_specs=(
            pl.BlockSpec((pieces, held, width), lambda i: (i, 0, 0)),
            pl.BlockSpec((8, width), lambda i: (0, 0)),
        ),
        compiler_params=pltpu.CompilerParams(vmem_limit_bytes=VMEM_LIMIT),
        cost_estimate=pl.CostEstimate(
            flops=6 * tokens * full_width,
            bytes_accessed=18 * tokens * full_width,
            transcendentals=0,
        ),
    )(timesteps, *arrays)


def attention_body(
    slot,
    block_rows,
    chunk,
    steps_ref,
    query_ref,
    key_ref,
    value_ref,
    field_ref,
    gate_ref,
    misfit_ref,
    out_ref,
    q_rows,
    k_rows,
    v_rows,
    k_cols,
    v_cols,
    field_cols,
    scores,
    weights,
    key_total,
    value_total,
    gate_total,
    misfit_total,
):
    length = q_rows.shape[0]
    pieces = out_ref.shape[1]
    tokens = length // pieces
    step_set = pl.program_id(0)
    scale_factor = HD ** (-0.5)
    log2e = 1.4426950408889634
    coefficient = step_coef(steps_ref[step_set, slot], (8, block_rows))[0:1]
    q_rows[...] = query_ref[...].reshape(length, HD)
    k_rows[...] = key_ref[...].reshape(length, HD)
    v_rows[...] = value_ref[...].reshape(length, HD)
    k_cols[...] = k_rows[...].T
    v_cols[...] = v_rows[...].T
    field_cols[...] = field_ref[...].reshape(length, HD).T
    gate_row = gate_ref[0, slot : slot + 1, :].astype(F32)
    gate = jnp.broadcast_to(gate_row, (8, HD)).T[:, 0:1]
    gate_total[...] = jnp.zeros_like(gate_total)
    misfit_total[...] = jnp.zeros_like(misfit_total)
    chunks = [slice(at, at + chunk) for at in range(0, length, chunk)]

    def one_block(index, _):
        first = index == 0
        start = pl.multiple_of(index * block_rows, block_rows)
        rows_query = q_rows[pl.ds(start, block_rows), :]
        top = jnp.full((8, block_rows), -jnp.inf, F32)
        for part in chunks:
            block_scores = dot(k_rows[part, :], rows_query, NT)
            scores[part, :] = block_scores
            top = jnp.maximum(top, fold_rows(block_scores, jnp.max))
        row_max = jnp.max(top, axis=0, keepdims=True)
        sums = jnp.zeros((8, block_rows), F32)
        for part in chunks:
            raised = jnp.exp2((scores[part, :] - row_max) * (scale_factor * log2e))
            sums = sums + fold_rows(raised, jnp.sum)
            scores[part, :] = raised
        inverse = 1.0 / jnp.sum(sums, axis=0, keepdims=True)
        mixed = jnp.zeros((HD, block_rows), F32)
        for part in chunks:
            rounded = (scores[part, :] * inverse).astype(BF16)
            weights[part, :] = rounded
            mixed = mixed + dot(v_cols[:, part], rounded)
        attended = mixed.astype(BF16).astype(F32)
        field = field_cols[:, pl.ds(start, block_rows)].astype(F32)
        moved = coefficient * (gate * attended)
        misfit_total[...] += moved * (2.0 * field + moved)
        grad_gap = coefficient * (field + moved)
        gate_total[...] += grad_gap * attended
        grad_cols = (grad_gap * gate).astype(BF16)
        grad_rows = grad_cols.T
        row_dot = jnp.sum(grad_cols.astype(F32) * attended, axis=0, keepdims=True)
        grad_query = jnp.zeros((HD, block_rows), F32)
        for part in chunks:
            rounded = weights[part, :]
            grad_probs = dot(v_rows[part, :], grad_cols)
            grad_scores = (rounded.astype(F32) * (grad_probs - row_dot)).astype(BF16)
            grad_query = grad_query + dot(k_cols[:, part], grad_scores)
            value_part = dot(rounded, grad_rows)
            key_part = dot(grad_scores, rows_query)
            value_total[part, :] = jnp.where(first, value_part, value_total[part, :] + value_part)
            key_total[part, :] = jnp.where(first, key_part, key_total[part, :] + key_part)
        held = block_rows // tokens
        out_ref[0, pl.ds(index * held, held), 0:tokens, :] = (
            (grad_query.T * scale_factor).astype(BF16).reshape(held, tokens, HD)
        )
        return 0

    lax.fori_loop(0, length // block_rows, one_block, 0)
    out_ref[0, :, tokens : 2 * tokens, :] = (
        (key_total[...] * scale_factor).astype(BF16).reshape(pieces, tokens, HD)
    )
    out_ref[0, :, 2 * tokens : 3 * tokens, :] = (
        value_total[...].astype(BF16).reshape(pieces, tokens, HD)
    )

    def row_of(values):
        total = values[:, 0:HD]
        for at in range(HD, values.shape[1], HD):
            total = total + values[:, at : at + HD]
        return jnp.sum(total.T, axis=0, keepdims=True)

    gate_row = row_of(gate_total[...])
    local_row = jnp.sum(misfit_ref[...], axis=0, keepdims=True)
    misfit_row = row_of(misfit_total[...]) + jnp.where(step_set == lax.axis_index("expert"), local_row, 0.0)
    rest = misfit_row
    side = []
    for _ in range(3):
        side.append(rest.astype(BF16).astype(F32))
        rest = rest - side[-1]
    gate_high = gate_row.astype(BF16).astype(F32)
    row_at = lax.broadcasted_iota(jnp.int32, (SIDE, HD), 0)
    rows = jnp.zeros((SIDE, HD), F32)
    for at, row in enumerate([gate_high, gate_row - gate_high] + side):
        rows = jnp.where(row_at == at, row, rows)
    out_ref[0, :, 3 * tokens :, :] = jnp.broadcast_to(
        rows.astype(BF16)[None], (pieces, SIDE, HD)
    )


def attention(slot, timesteps, arrived, gates, misfit):
    sets, groups, _, width = arrived.shape
    tokens = arrived.shape[2] // 4
    length = groups * tokens
    block_rows, chunk = 512, 512

    def field(which):
        return pl.BlockSpec((1, groups, tokens, HD), lambda e: (e, 0, which, 0))

    return pl.pallas_call(
        functools.partial(attention_body, slot, block_rows, chunk),
        grid=(sets,),
        out_shape=jax.ShapeDtypeStruct((sets, groups, 3 * tokens + SIDE, width), BF16),
        in_specs=[pl.BlockSpec(memory_space=pltpu.SMEM)]
        + [field(which) for which in range(4)]
        + [
            pl.BlockSpec((1,) + gates.shape[1:], lambda e: (e, 0, 0)),
            pl.BlockSpec((8, HD), lambda e: (0, 0)),
        ],
        out_specs=pl.BlockSpec((1, groups, 3 * tokens + SIDE, HD), lambda e: (e, 0, 0, 0)),
        scratch_shapes=[pltpu.VMEM((length, HD), BF16)] * 3
        + [pltpu.VMEM((HD, length), BF16)] * 3
        + [
            pltpu.VMEM((length, block_rows), F32),
            pltpu.VMEM((length, block_rows), BF16),
            pltpu.VMEM((length, HD), F32),
            pltpu.VMEM((length, HD), F32),
            pltpu.VMEM((HD, block_rows), F32),
            pltpu.VMEM((HD, block_rows), F32),
        ],
        compiler_params=pltpu.CompilerParams(vmem_limit_bytes=VMEM_LIMIT),
        cost_estimate=pl.CostEstimate(
            flops=sets * 24 * length * length * HD,
            bytes_accessed=sets * 14 * length * width,
            transcendentals=sets * length * length,
        ),
    )(timesteps, arrived, arrived, arrived, arrived, gates, misfit)


def unpack_body(slot, entries, weight_ref, kept_ref, main_ref, side_ref, *refs):
    query_ref, key_ref, value_ref, gate_ref, log_ref = refs[-5:]
    earlier = refs[:-5]
    pieces = main_ref.shape[0]
    width = main_ref.shape[2]
    tokens = query_ref.shape[2]
    misfit = jnp.sum(side_ref[:, 2:5, :].astype(F32))
    ratio_log = jnp.full((1, HD), -misfit / (2.0 * entries), F32)
    if earlier:
        gate_ref[0, 0:1, :] = earlier[0][...].astype(BF16)
        own_log = ratio_log[:, 0:1] * kept_ref[slot]
        log_ref[...] = jnp.concatenate([earlier[1][:, 0:1], own_log], axis=1).astype(BF16)
    else:
        log_ref[...] = ratio_log * kept_ref[slot]
    factor = weight_ref[slot] * jnp.exp(ratio_log)
    first = pl.program_id(0) * pieces
    for piece in range(pieces):
        columns = slice(piece * width, (piece + 1) * width)
        parts = side_ref[first + piece, 0:2, :].astype(F32)
        gate_row = (parts[0:1] + parts[1:2]) * factor
        if earlier:
            gate_ref[0, 1:2, columns] = gate_row.astype(BF16)
        else:
            gate_ref[:, columns] = gate_row
        for which, out_ref in enumerate((query_ref, key_ref, value_ref)):
            rows = main_ref[piece, which * tokens : (which + 1) * tokens, :].astype(F32)
            out_ref[0, 0, :, columns] = (rows * factor).astype(BF16)


def unpack(slot, slots, weight, kept, returned, previous):
    heads, rows, width = returned.shape
    tokens = (rows - SIDE) // 3
    full_width = heads * width
    entries = full_width * tokens * lax.axis_size("seq")
    pieces = 16
    whole = jax.ShapeDtypeStruct((1, slots, tokens, full_width), BF16)
    part = pl.BlockSpec((1, 1, tokens, pieces * width), lambda i: (0, slot, 0, i))
    in_specs = [
        pl.BlockSpec(memory_space=pltpu.SMEM),
        pl.BlockSpec(memory_space=pltpu.SMEM),
        pl.BlockSpec((pieces, 3 * tokens, width), lambda i: (i, 0, 0)),
        pl.BlockSpec((heads, SIDE, width), lambda i: (0, 3 * tokens // SIDE, 0)),
    ]
    if previous:
        in_specs += [pl.BlockSpec(memory_space=pl.ANY)] * 3 + [
            pl.BlockSpec((1, pieces * width), lambda i: (0, i)),
            pl.BlockSpec((1, HD), lambda i: (0, 0)),
        ]
        small = (
            jax.ShapeDtypeStruct((1, slots, full_width), BF16),
            jax.ShapeDtypeStruct((1, slots), BF16),
        )
        small_specs = (
            pl.BlockSpec((1, slots, pieces * width), lambda i: (0, 0, i)),
            pl.BlockSpec((1, slots), lambda i: (0, 0)),
        )
    else:
        small = (
            jax.ShapeDtypeStruct((1, full_width), F32),
            jax.ShapeDtypeStruct((1, HD), F32),
        )
        small_specs = (
            pl.BlockSpec((1, pieces * width), lambda i: (0, i)),
            pl.BlockSpec((1, HD), lambda i: (0, 0)),
        )

    def body(weight_ref, kept_ref, main_ref, side_ref, *refs):
        refs = refs[3:] if previous else refs
        unpack_body(slot, entries, weight_ref, kept_ref, main_ref, side_ref, *refs)

    return pl.pallas_call(
        body,
        grid=(heads // pieces,),
        out_shape=(whole, whole, whole) + small,
        in_specs=in_specs,
        out_specs=(part, part, part) + small_specs,
        input_output_aliases={4 + at: at for at in range(3)} if previous else {},
        compiler_params=pltpu.CompilerParams(vmem_limit_bytes=UNPACK_LIMIT),
        cost_estimate=pl.CostEstimate(
            flops=3 * tokens * full_width,
            bytes_accessed=12 * tokens * full_width,
            transcendentals=0,
        ),
    )(weight, kept, returned, returned, *previous)


def exchange(pieces):
    return lax.all_to_all(pieces, ("expert", "seq"), split_axis=0, concat_axis=0, tiled=True)


def sum_over_replicas(values):
    replicas = lax.axis_size("rep")
    total = values
    for shift in range(1, replicas):
        total = total + lax.ppermute(
            values, "rep", [(at, (at + shift) % replicas) for at in range(replicas)]
        )
    return total


def local(
    query_in,
    key_in,
    value_in,
    sample_noise,
    old_velocity,
    gate_scale,
    rewards,
    group_ids,
    timesteps,
    counts,
):
    slots = query_in.shape[1]
    tokens = query_in.shape[2]
    full_width = query_in.shape[3]
    groups = lax.axis_size("seq")
    sets = lax.axis_size("expert")
    heads = sets * groups
    width = full_width // heads
    expert_at = lax.axis_index("expert")

    def own_expert(both):
        return lax.dynamic_index_in_dim(both, expert_at, 0, keepdims=False)

    arrays = (query_in, key_in, value_in, sample_noise, old_velocity)
    kept_mask = (
        jnp.arange(slots, dtype=jnp.int32)[None, :] < counts[:, 0][:, None]
    ).astype(F32)
    choose = (group_ids[..., None] == jnp.arange(GROUPS, dtype=jnp.int32)).astype(F32)
    live_mask = choose * kept_mask[..., None]
    sums = sum_over_replicas(
        jnp.stack(
            (
                jnp.sum(live_mask, axis=(0, 1)),
                jnp.sum(live_mask * rewards[..., None], axis=(0, 1)),
                jnp.sum(live_mask * (rewards * rewards)[..., None], axis=(0, 1)),
            )
        )
    )
    number, reward_sum, square = sums[0], sums[1], sums[2]
    group_mean = reward_sum / jnp.maximum(number, 1.0)
    spread = square / jnp.maximum(number, 1.0) - group_mean * group_mean
    centre = jnp.sum(choose * group_mean, axis=-1)
    group_scale = jnp.sum(choose * jnp.sqrt(jnp.maximum(spread, 1.0)), axis=-1)
    advantage = (rewards - centre) / group_scale
    kept_here = own_expert(kept_mask)
    weight = own_expert(kept_mask * advantage)

    gate_own = gate_scale[0]
    gate_other = lax.ppermute(gate_own, "expert", [(0, 1), (1, 0)])
    arrived, misfits = [], []
    for slot in range(slots):
        packed, misfit = pack(slot, timesteps, arrays, heads)
        if slot == 1:
            packed, gate_other = lax.optimization_barrier((packed, gate_other))
        arrived.append(exchange(packed).reshape((sets, groups) + packed.shape[1:]))
        misfits.append(misfit)
    gates = jnp.where(
        expert_at == 0, jnp.stack([gate_own, gate_other]), jnp.stack([gate_other, gate_own])
    )
    head_at = expert_at * groups + lax.axis_index("seq")
    gates = lax.dynamic_slice_in_dim(gates, head_at * width, width, 2)
    returned = []
    for slot in range(slots):
        sent = attention(
            slot, timesteps, arrived[slot], gates, misfits[slot]
        )
        returned.append(exchange(sent.reshape(heads, 3 * tokens + SIDE, width)))
    held = ()
    for slot in range(slots):
        held = unpack(slot, slots, weight, kept_here, returned[slot], held)
    return held


def solution(mesh):
    placed = (
        P("expert", "rep", "seq", None),
        P("expert", "rep", "seq", None),
        P("expert", "rep", "seq", None),
        P("expert", "rep", "seq", None),
        P("expert", "rep", "seq", None),
        P("expert", "rep", None),
        P(None, "rep"),
        P(None, "rep"),
        P(None, "rep"),
        P(None, "rep"),
    )
    return jax.shard_map(
        local,
        mesh=mesh,
        in_specs=placed,
        out_specs=(
            P("expert", "rep", "seq", None),
            P("expert", "rep", "seq", None),
            P("expert", "rep", "seq", None),
            P("expert", "rep", None),
            P("expert", "rep"),
        ),
        check_vma=False,
    )
```

```python
import functools

import jax
import jax.numpy as jnp
from jax import lax
from jax.experimental import pallas as pl
from jax.experimental.pallas import tpu as pltpu
from jax.sharding import PartitionSpec as P

HD = 128
GROUPS = 4
SIDE = 16
F32 = jnp.float32
BF16 = jnp.bfloat16
NN = (((1,), (0,)), ((), ()))
NT = (((1,), (1,)), ((), ()))
VMEM_LIMIT = 63 * 1024 * 1024
ATTENTION_LIMIT = 56 * 1024 * 1024
UNPACK_LIMIT = 24 * 1024 * 1024


def step_coef(timestep, shape):
    fraction = jnp.full(shape, timestep.astype(F32)) / 1000.0
    sigma_level = 0.7 * jnp.sqrt(fraction / (1.0 - fraction))
    return jnp.sqrt(jnp.float32(0.1)) / sigma_level


def dot(left, right, dims=NN):
    return lax.dot_general(left, right, dims, preferred_element_type=F32)


def fold_rows(values, reduce):
    rows, columns = values.shape
    return reduce(values.reshape(rows // 8, 8, columns), axis=0)


def pack_body(
    slot, steps_ref, query_ref, key_ref, value_ref, noise_ref, old_ref, out_ref, misfit_ref
):
    pieces, _, width = out_ref.shape
    tokens = query_ref.shape[2]
    coefficient = step_coef(steps_ref[lax.axis_index("expert"), slot], (8, width))[0:1]

    @pl.when(pl.program_id(0) == 0)
    def _():
        misfit_ref[...] = jnp.zeros_like(misfit_ref)

    total = misfit_ref[...]
    for piece in range(pieces):
        columns = slice(piece * width, (piece + 1) * width)
        out_ref[piece, 0:tokens] = query_ref[0, 0, :, columns]
        out_ref[piece, tokens : 2 * tokens] = key_ref[0, 0, :, columns]
        out_ref[piece, 2 * tokens : 3 * tokens] = value_ref[0, 0, :, columns]
        noise = noise_ref[0, 0, :, columns].astype(F32)
        shift = coefficient * old_ref[0, 0, :, columns].astype(F32)
        out_ref[piece, 3 * tokens : 4 * tokens] = (noise - shift).astype(BF16)
        total = total + fold_rows(shift * (shift - 2.0 * noise), jnp.sum)
    misfit_ref[...] = total


def pack(slot, timesteps, arrays, groups):
    _, _, tokens, full_width = arrays[0].shape
    width = full_width // groups
    pieces = 16
    rows = pl.BlockSpec((1, 1, tokens, pieces * width), lambda i: (0, slot, 0, i))
    held = 4 * tokens
    return pl.pallas_call(
        functools.partial(pack_body, slot),
        grid=(groups // pieces,),
        out_shape=(
            jax.ShapeDtypeStruct((groups, held, width), BF16),
            jax.ShapeDtypeStruct((8, width), F32),
        ),
        in_specs=[pl.BlockSpec(memory_space=pltpu.SMEM)] + [rows] * 5,
        out_specs=(
            pl.BlockSpec((pieces, held, width), lambda i: (i, 0, 0)),
            pl.BlockSpec((8, width), lambda i: (0, 0)),
        ),
        compiler_params=pltpu.CompilerParams(vmem_limit_bytes=VMEM_LIMIT),
        cost_estimate=pl.CostEstimate(
            flops=6 * tokens * full_width,
            bytes_accessed=18 * tokens * full_width,
            transcendentals=0,
        ),
    )(timesteps, *arrays)


def attention_body(
    slot,
    block_rows,
    chunk,
    steps_ref,
    query_ref,
    key_ref,
    value_ref,
    field_ref,
    gate_ref,
    misfit_ref,
    out_ref,
    q_rows,
    k_rows,
    v_rows,
    k_cols,
    v_cols,
    field_cols,
    scores,
    weights,
    key_total,
    value_total,
    gate_total,
    misfit_total,
):
    length = q_rows.shape[0]
    pieces = out_ref.shape[1]
    tokens = length // pieces
    step_set = pl.program_id(0)
    scale_factor = HD ** (-0.5)
    log2e = 1.4426950408889634
    coefficient = step_coef(steps_ref[step_set, slot], (8, block_rows))[0:1]
    q_rows[...] = query_ref[...].reshape(length, HD)
    k_rows[...] = key_ref[...].reshape(length, HD)
    v_rows[...] = value_ref[...].reshape(length, HD)
    k_cols[...] = k_rows[...].T
    v_cols[...] = v_rows[...].T
    field_cols[...] = field_ref[...].reshape(length, HD).T
    gate_row = gate_ref[0, slot : slot + 1, :].astype(F32)
    gate = jnp.broadcast_to(gate_row, (8, HD)).T[:, 0:1]
    gate_total[...] = jnp.zeros_like(gate_total)
    misfit_total[...] = jnp.zeros_like(misfit_total)
    chunks = [slice(at, at + chunk) for at in range(0, length, chunk)]

    def one_block(index, _):
        first = index == 0
        start = pl.multiple_of(index * block_rows, block_rows)
        rows_query = q_rows[pl.ds(start, block_rows), :]
        top = jnp.full((8, block_rows), -jnp.inf, F32)
        for part in chunks:
            block_scores = dot(k_rows[part, :], rows_query, NT)
            scores[part, :] = block_scores
            top = jnp.maximum(top, fold_rows(block_scores, jnp.max))
        row_max = jnp.max(top, axis=0, keepdims=True)
        sums = jnp.zeros((8, block_rows), F32)
        for part in chunks:
            raised = jnp.exp2((scores[part, :] - row_max) * (scale_factor * log2e))
            sums = sums + fold_rows(raised, jnp.sum)
            scores[part, :] = raised
        inverse = 1.0 / jnp.sum(sums, axis=0, keepdims=True)
        mixed = jnp.zeros((HD, block_rows), F32)
        for part in chunks:
            rounded = (scores[part, :] * inverse).astype(BF16)
            weights[part, :] = rounded
            mixed = mixed + dot(v_cols[:, part], rounded)
        attended = mixed.astype(BF16).astype(F32)
        field = field_cols[:, pl.ds(start, block_rows)].astype(F32)
        moved = coefficient * (gate * attended)
        misfit_total[...] += moved * (2.0 * field + moved)
        grad_gap = coefficient * (field + moved)
        gate_total[...] += grad_gap * attended
        grad_cols = (grad_gap * gate).astype(BF16)
        grad_rows = grad_cols.T
        row_dot = jnp.sum(grad_cols.astype(F32) * attended, axis=0, keepdims=True)
        grad_query = jnp.zeros((HD, block_rows), F32)
        for part in chunks:
            rounded = weights[part, :]
            grad_probs = dot(v_rows[part, :], grad_cols)
            grad_scores = (rounded.astype(F32) * (grad_probs - row_dot)).astype(BF16)
            grad_query = grad_query + dot(k_cols[:, part], grad_scores)
            value_part = dot(rounded, grad_rows)
            key_part = dot(grad_scores, rows_query)
            value_total[part, :] = jnp.where(first, value_part, value_total[part, :] + value_part)
            key_total[part, :] = jnp.where(first, key_part, key_total[part, :] + key_part)
        held = block_rows // tokens
        out_ref[0, pl.ds(index * held, held), 0:tokens, :] = (
            (grad_query.T * scale_factor).astype(BF16).reshape(held, tokens, HD)
        )
        return 0

    lax.fori_loop(0, length // block_rows, one_block, 0)
    out_ref[0, :, tokens : 2 * tokens, :] = (
        (key_total[...] * scale_factor).astype(BF16).reshape(pieces, tokens, HD)
    )
    out_ref[0, :, 2 * tokens : 3 * tokens, :] = (
        value_total[...].astype(BF16).reshape(pieces, tokens, HD)
    )

    def row_of(values):
        total = values[:, 0:HD]
        for at in range(HD, values.shape[1], HD):
            total = total + values[:, at : at + HD]
        return jnp.sum(total.T, axis=0, keepdims=True)

    gate_row = row_of(gate_total[...])
    local_row = jnp.sum(misfit_ref[...], axis=0, keepdims=True)
    misfit_row = row_of(misfit_total[...]) + jnp.where(step_set == lax.axis_index("expert"), local_row, 0.0)
    rest = misfit_row
    side = []
    for _ in range(3):
        side.append(rest.astype(BF16).astype(F32))
        rest = rest - side[-1]
    gate_high = gate_row.astype(BF16).astype(F32)
    row_at = lax.broadcasted_iota(jnp.int32, (SIDE, HD), 0)
    rows = jnp.zeros((SIDE, HD), F32)
    for at, row in enumerate([gate_high, gate_row - gate_high] + side):
        rows = jnp.where(row_at == at, row, rows)
    out_ref[0, :, 3 * tokens :, :] = jnp.broadcast_to(
        rows.astype(BF16)[None], (pieces, SIDE, HD)
    )


def attention(slot, timesteps, arrived, gates, misfit):
    sets, groups, _, width = arrived.shape
    tokens = arrived.shape[2] // 4
    length = groups * tokens
    block_rows, chunk = 512, 512

    def field(which):
        return pl.BlockSpec((1, groups, tokens, HD), lambda e: (e, 0, which, 0))

    return pl.pallas_call(
        functools.partial(attention_body, slot, block_rows, chunk),
        grid=(sets,),
        out_shape=jax.ShapeDtypeStruct((sets, groups, 3 * tokens + SIDE, width), BF16),
        in_specs=[pl.BlockSpec(memory_space=pltpu.SMEM)]
        + [field(which) for which in range(4)]
        + [
            pl.BlockSpec((1,) + gates.shape[1:], lambda e: (e, 0, 0)),
            pl.BlockSpec((8, HD), lambda e: (0, 0)),
        ],
        out_specs=pl.BlockSpec((1, groups, 3 * tokens + SIDE, HD), lambda e: (e, 0, 0, 0)),
        scratch_shapes=[pltpu.VMEM((length, HD), BF16)] * 3
        + [pltpu.VMEM((HD, length), BF16)] * 3
        + [
            pltpu.VMEM((length, block_rows), F32),
            pltpu.VMEM((length, block_rows), BF16),
            pltpu.VMEM((length, HD), F32),
            pltpu.VMEM((length, HD), F32),
            pltpu.VMEM((HD, block_rows), F32),
            pltpu.VMEM((HD, block_rows), F32),
        ],
        compiler_params=pltpu.CompilerParams(vmem_limit_bytes=ATTENTION_LIMIT),
        cost_estimate=pl.CostEstimate(
            flops=sets * 24 * length * length * HD,
            bytes_accessed=sets * 14 * length * width,
            transcendentals=sets * length * length,
        ),
    )(timesteps, arrived, arrived, arrived, arrived, gates, misfit)


def unpack_body(slot, entries, weight_ref, kept_ref, main_ref, side_ref, *refs):
    query_ref, key_ref, value_ref, gate_ref, log_ref = refs[-5:]
    earlier = refs[:-5]
    pieces = main_ref.shape[0]
    width = main_ref.shape[2]
    tokens = query_ref.shape[2]
    misfit = jnp.sum(side_ref[:, 2:5, :].astype(F32))
    ratio_log = jnp.full((1, HD), -misfit / (2.0 * entries), F32)
    if earlier:
        gate_ref[0, 0:1, :] = earlier[0][...].astype(BF16)
        own_log = ratio_log[:, 0:1] * kept_ref[slot]
        log_ref[...] = jnp.concatenate([earlier[1][:, 0:1], own_log], axis=1).astype(BF16)
    else:
        log_ref[...] = ratio_log * kept_ref[slot]
    factor = weight_ref[slot] * jnp.exp(ratio_log)
    first = pl.program_id(0) * pieces
    for piece in range(pieces):
        columns = slice(piece * width, (piece + 1) * width)
        parts = side_ref[first + piece, 0:2, :].astype(F32)
        gate_row = (parts[0:1] + parts[1:2]) * factor
        if earlier:
            gate_ref[0, 1:2, columns] = gate_row.astype(BF16)
        else:
            gate_ref[:, columns] = gate_row
        for which, out_ref in enumerate((query_ref, key_ref, value_ref)):
            rows = main_ref[piece, which * tokens : (which + 1) * tokens, :].astype(F32)
            out_ref[0, 0, :, columns] = (rows * factor).astype(BF16)


def unpack(slot, slots, weight, kept, returned, previous):
    heads, rows, width = returned.shape
    tokens = (rows - SIDE) // 3
    full_width = heads * width
    entries = full_width * tokens * lax.axis_size("seq")
    pieces = 16
    whole = jax.ShapeDtypeStruct((1, slots, tokens, full_width), BF16)
    part = pl.BlockSpec((1, 1, tokens, pieces * width), lambda i: (0, slot, 0, i))
    in_specs = [
        pl.BlockSpec(memory_space=pltpu.SMEM),
        pl.BlockSpec(memory_space=pltpu.SMEM),
        pl.BlockSpec((pieces, 3 * tokens, width), lambda i: (i, 0, 0)),
        pl.BlockSpec((heads, SIDE, width), lambda i: (0, 3 * tokens // SIDE, 0)),
    ]
    if previous:
        in_specs += [pl.BlockSpec(memory_space=pl.ANY)] * 3 + [
            pl.BlockSpec((1, pieces * width), lambda i: (0, i)),
            pl.BlockSpec((1, HD), lambda i: (0, 0)),
        ]
        small = (
            jax.ShapeDtypeStruct((1, slots, full_width), BF16),
            jax.ShapeDtypeStruct((1, slots), BF16),
        )
        small_specs = (
            pl.BlockSpec((1, slots, pieces * width), lambda i: (0, 0, i)),
            pl.BlockSpec((1, slots), lambda i: (0, 0)),
        )
    else:
        small = (
            jax.ShapeDtypeStruct((1, full_width), F32),
            jax.ShapeDtypeStruct((1, HD), F32),
        )
        small_specs = (
            pl.BlockSpec((1, pieces * width), lambda i: (0, i)),
            pl.BlockSpec((1, HD), lambda i: (0, 0)),
        )

    def body(weight_ref, kept_ref, main_ref, side_ref, *refs):
        refs = refs[3:] if previous else refs
        unpack_body(slot, entries, weight_ref, kept_ref, main_ref, side_ref, *refs)

    return pl.pallas_call(
        body,
        grid=(heads // pieces,),
        out_shape=(whole, whole, whole) + small,
        in_specs=in_specs,
        out_specs=(part, part, part) + small_specs,
        input_output_aliases={4 + at: at for at in range(3)} if previous else {},
        compiler_params=pltpu.CompilerParams(vmem_limit_bytes=UNPACK_LIMIT),
        cost_estimate=pl.CostEstimate(
            flops=3 * tokens * full_width,
            bytes_accessed=12 * tokens * full_width,
            transcendentals=0,
        ),
    )(weight, kept, returned, returned, *previous)


def exchange(pieces):
    return lax.all_to_all(pieces, ("expert", "seq"), split_axis=0, concat_axis=0, tiled=True)


def sum_over_replicas(values):
    replicas = lax.axis_size("rep")
    total = values
    for shift in range(1, replicas):
        total = total + lax.ppermute(
            values, "rep", [(at, (at + shift) % replicas) for at in range(replicas)]
        )
    return total


def local(
    query_in,
    key_in,
    value_in,
    sample_noise,
    old_velocity,
    gate_scale,
    rewards,
    group_ids,
    timesteps,
    counts,
):
    slots = query_in.shape[1]
    tokens = query_in.shape[2]
    full_width = query_in.shape[3]
    groups = lax.axis_size("seq")
    sets = lax.axis_size("expert")
    heads = sets * groups
    width = full_width // heads
    expert_at = lax.axis_index("expert")

    def own_expert(both):
        return lax.dynamic_index_in_dim(both, expert_at, 0, keepdims=False)

    arrays = (query_in, key_in, value_in, sample_noise, old_velocity)
    kept_mask = (
        jnp.arange(slots, dtype=jnp.int32)[None, :] < counts[:, 0][:, None]
    ).astype(F32)
    choose = (group_ids[..., None] == jnp.arange(GROUPS, dtype=jnp.int32)).astype(F32)
    live_mask = choose * kept_mask[..., None]
    sums = sum_over_replicas(
        jnp.stack(
            (
                jnp.sum(live_mask, axis=(0, 1)),
                jnp.sum(live_mask * rewards[..., None], axis=(0, 1)),
                jnp.sum(live_mask * (rewards * rewards)[..., None], axis=(0, 1)),
            )
        )
    )
    number, reward_sum, square = sums[0], sums[1], sums[2]
    group_mean = reward_sum / jnp.maximum(number, 1.0)
    spread = square / jnp.maximum(number, 1.0) - group_mean * group_mean
    centre = jnp.sum(choose * group_mean, axis=-1)
    group_scale = jnp.sum(choose * jnp.sqrt(jnp.maximum(spread, 1.0)), axis=-1)
    advantage = (rewards - centre) / group_scale
    kept_here = own_expert(kept_mask)
    weight = own_expert(kept_mask * advantage)

    gate_own = gate_scale[0]
    gate_other = lax.ppermute(gate_own, "expert", [(0, 1), (1, 0)])
    arrived, misfits = [], []
    for slot in range(slots):
        packed, misfit = pack(slot, timesteps, arrays, heads)
        if slot == 1:
            packed, gate_other = lax.optimization_barrier((packed, gate_other))
        arrived.append(exchange(packed).reshape((sets, groups) + packed.shape[1:]))
        misfits.append(misfit)
    gates = jnp.where(
        expert_at == 0, jnp.stack([gate_own, gate_other]), jnp.stack([gate_other, gate_own])
    )
    head_at = expert_at * groups + lax.axis_index("seq")
    gates = lax.dynamic_slice_in_dim(gates, head_at * width, width, 2)
    returned = []
    for slot in range(slots):
        sent = attention(
            slot, timesteps, arrived[slot], gates, misfits[slot]
        )
        returned.append(exchange(sent.reshape(heads, 3 * tokens + SIDE, width)))
    held = ()
    for slot in range(slots):
        held = unpack(slot, slots, weight, kept_here, returned[slot], held)
    return held


def solution(mesh):
    placed = (
        P("expert", "rep", "seq", None),
        P("expert", "rep", "seq", None),
        P("expert", "rep", "seq", None),
        P("expert", "rep", "seq", None),
        P("expert", "rep", "seq", None),
        P("expert", "rep", None),
        P(None, "rep"),
        P(None, "rep"),
        P(None, "rep"),
        P(None, "rep"),
    )
    return jax.shard_map(
        local,
        mesh=mesh,
        in_specs=placed,
        out_specs=(
            P("expert", "rep", "seq", None),
            P("expert", "rep", "seq", None),
            P("expert", "rep", "seq", None),
            P("expert", "rep", None),
            P("expert", "rep"),
        ),
        check_vma=False,
    )
```
